32 devices in a mesh: track: 8 (over y, x, core), strip: 4 (over z).
Axes of the slice: x: 2, y: 2, z: 4, core: 2. Of those that a mesh axis runs over, the one named last changes fastest.
Arguments:
- rhs: float32 [4, 128, 256], P('strip', 'track'), may hold values from -6 to 6
- principal_tiles: bfloat16 [4, 128, 256, 256], P('strip', 'track')
- lower_blocks: bfloat16 [4, 128, 256, 256], P('strip', 'track')
- coupling_blocks: bfloat16 [4, 128, 256, 256], P('strip', 'track'), may hold values from -0.09375 to 0.09375
- precond_blocks: bfloat16 [4, 128, 256, 256], P('strip', 'track'), as said below
- seg_blocks: int32 [8], P('track'), may hold values from 1 to 16, 80 in all
- links: int32 [4, 128], P('strip', 'track'), may hold values 0 or 1
Outputs:
- solution: float32 [4, 128, 256], P('strip', 'track')
- residual: float32 [4, 128, 256], P('strip', 'track')
The draws below stay inside these ranges and needn't reach their ends.
Inputs may be any that keep to these rules, and one draw needn't show every extreme that they name: `seg_blocks`: each device holds at least one live block and the counts of all devices sum to 80. `precond_blocks`: approximate inverses of the diagonal blocks.
All inputs are finite; a program needn't handle non-finite values. No bound on the sum of `links` on one device may be relied on, other than what follows from the above.
Results may differ from the reference program's by a relative error of at most 0.0004.
Values sent between devices are 32-bit elements; how exact they have to be, the bound alone decides.
No kernel may reach another device: no remote copies, remote signals or barrier semaphores. Data moves between devices by JAX's collectives and lax.ppermute only.
A program may use at most 128 MiB of HBM per device.

```python
import math
import jax
import jax.numpy as jnp
import numpy as np
from jax import lax

B = 256
CAP = 16
ITERS = 6
BAND_ACTIVE_TILES = 80
N_TRACK = 8
N_STRIP = 4


coupled_noise = 0.25


inverse_noise = 0.1


lower_noise = 0.2


def noise_field(key, tag):
    shape = (N_STRIP, N_TRACK * CAP, B, B)
    sub = jax.random.fold_in(key, tag)
    values = jax.random.normal(sub, shape, jnp.float32)
    return values / math.sqrt(B)


def block_scales(key):
    sub = jax.random.fold_in(key, 21)
    rows = N_TRACK * CAP
    return jnp.exp(jax.random.uniform(sub, (N_STRIP, rows), jnp.float32, math.log(3.0), math.log(8.0)))


def identity_block():
    index = jnp.arange(B)
    return (index[:, None] == index[None, :]).astype(jnp.float32)


def decay_field(key):
    rows = N_TRACK * CAP
    bottom = math.log(0.25 / BAND_ACTIVE_TILES)
    top = math.log(max(0.04, 2.0 / BAND_ACTIVE_TILES))
    falloff_speed = jnp.exp(jax.random.uniform(jax.random.fold_in(key, 31), (N_STRIP, 1, B), jnp.float32, bottom, top))
    extent_across = jnp.exp(jax.random.uniform(jax.random.fold_in(key, 32), (N_STRIP, rows, B), jnp.float32, math.log(0.5), math.log(2.0)))
    chosen_position = jax.random.uniform(jax.random.fold_in(key, 33), (N_STRIP, rows, 1), jnp.float32)
    pass_levels_number = jax.random.uniform(jax.random.fold_in(key, 34), (N_STRIP, rows, 1), jnp.float32, 0.5, 0.8)
    pulse_total = jnp.where(chosen_position < 3.0 / BAND_ACTIVE_TILES, pass_levels_number, 1.0)
    return jnp.exp(-falloff_speed * extent_across) * pulse_total


def draw_principal_tiles(key, part):
    scales = block_scales(key)
    coupled = noise_field(key, 41)
    outcome = scales[:, :, None, None] * (identity_block()[None, None] + coupled_noise * coupled)
    return outcome.astype(jnp.bfloat16)


def draw_precond_blocks(key, part):
    scales = block_scales(key)
    coupled = noise_field(key, 41)
    extra = noise_field(key, 42)
    outcome = (identity_block()[None, None] - coupled_noise * coupled + inverse_noise * extra) / scales[:, :, None, None]
    return outcome.astype(jnp.bfloat16)


def draw_lower_blocks(key, part):
    scales = block_scales(key)
    mixing = noise_field(key, 43)
    decay = decay_field(key)
    norming = math.sqrt((1.0 + coupled_noise ** 2 + inverse_noise ** 2) * (1.0 + lower_noise ** 2))
    outcome = -scales[:, :, None, None] * (identity_block()[None, None] + lower_noise * mixing) * decay[:, :, None, :] / norming
    return outcome.astype(jnp.bfloat16)


def place_ends(drawn, key, low, top_value):
    longest = drawn.shape.index(max(drawn.shape))
    spots = []
    for shift in (0, 1):
        where = [jax.random.randint(jax.random.fold_in(key, axis), (), 0, length) for axis, length in enumerate(drawn.shape)]
        where[longest] = (where[longest] + shift) % drawn.shape[longest]
        spots.append(tuple(where))
    return drawn.at[spots[0]].set(low).at[spots[1]].set(top_value)


def block_levels(rng, shape, shards, least, largest):
    factor_of = 1.0
    for dim, shards_of in shards:
        steps = jax.random.uniform(jax.random.fold_in(jax.random.fold_in(rng, 6), dim), (shards_of,), jnp.float32, least / len(shards), largest / len(shards))
        factor_of = factor_of * jnp.repeat(jnp.exp(steps), shape[dim] // shards_of).reshape((-1,) + (1,) * (len(shape) - 1 - dim))
    return factor_of


def split_up(amount, total, most, lean):
    weights = [(1 << 20) // math.isqrt(standing ** lean) + 1 for standing in range(2, amount + 1)]
    rest, given = total - most - (amount - 1), [1] * (amount - 1)
    while rest > 0:
        movable = [i for i in range(amount - 1) if given[i] < most]
        pool, left = sum([weights[i] for i in movable]), rest
        for i in movable:
            addition = min(most - given[i], max(1, left * weights[i] // pool), rest)
            given[i] = given[i] + addition
            rest = rest - addition
    return np.array([most] + given)


def ragged_sizes(stream_key, count, total, reach, lean):
    if count == 2:
        one = jax.random.randint(stream_key, (), max(1, total - reach), min(reach, total - 1) + 1)
        return jnp.stack([one, total - one])
    tallies = jnp.asarray(split_up(count, total, reach, lean), jnp.int32)
    couples = (count - 1) // 2
    donor, sink = tallies[1:1 + 2 * couples:2], tallies[2:2 + 2 * couples:2]
    margin = jnp.minimum(donor - 1, reach - sink)
    shifted = jax.random.randint(jax.random.fold_in(stream_key, 1), (couples,), 0, 1 << 20) % (margin + 1)
    tallies = tallies.at[1:1 + 2 * couples:2].set(donor - shifted).at[2:2 + 2 * couples:2].set(sink + shifted)
    return tallies[jax.random.permutation(jax.random.fold_in(stream_key, 2), count)]


def scatter_about(rng, extent, scale, bound, cuts=(), kind=jnp.bfloat16):
    array = scale * jax.random.normal(rng, extent, jnp.float32)
    if cuts:
        array = array * block_levels(rng, extent, cuts, -0.22, 0.18)
    return jnp.clip(array, -bound, bound).astype(kind)


def setup_inputs(seed: int = 0) -> dict:
    key_list = jax.random.split(jax.random.key(seed), 8)
    return {
        "rhs": scatter_about(key_list[0], (N_STRIP, N_TRACK * CAP, B), 1.0, 6.0, ((0, 4), (1, 8)), jnp.float32),
        "principal_tiles": draw_principal_tiles(jax.random.fold_in(key_list[7], 71), 0),
        "lower_blocks": draw_lower_blocks(jax.random.fold_in(key_list[7], 71), 0),
        "coupling_blocks": scatter_about(key_list[3], (N_STRIP, N_TRACK * CAP, B, B), (16 * B) ** -0.5, 0.09375, ((0, 4), (1, 8))),
        "precond_blocks": draw_precond_blocks(jax.random.fold_in(key_list[7], 71), 0),
        "seg_blocks": ragged_sizes(key_list[5], N_TRACK, BAND_ACTIVE_TILES, CAP, 2).astype(jnp.int32),
        "links": place_ends((jax.random.randint(key_list[6], (N_STRIP, N_TRACK * CAP), 0, 128) < 127).astype(jnp.int32), jax.random.fold_in(key_list[6], 1), 0, 1),
    }


def apply_blocks(mats, vecs):
    def one(pair):
        return jnp.einsum('kab,kb->ka', pair[0].astype(jnp.float32), pair[1], precision=lax.Precision.HIGHEST)
    return lax.map(one, (mats, vecs))


def apply_transposed(mats, vecs):
    def one(pair):
        return jnp.einsum('kba,kb->ka', pair[0].astype(jnp.float32), pair[1], precision=lax.Precision.HIGHEST)
    return lax.map(one, (mats, vecs))


def reference(rhs, principal_tiles, lower_blocks, coupling_blocks, precond_blocks, seg_blocks, links):
    strips, slots_all, width = rhs.shape
    flat = jnp.arange(slots_all, dtype=jnp.int32)
    slot = flat % CAP
    device = flat // CAP
    count = seg_blocks[device]
    live = slot < count
    prev_count = seg_blocks[jnp.maximum(device - 1, 0)]
    prev_index = jnp.where(slot > 0, flat - 1, (device - 1) * CAP + prev_count - 1)
    prev_index = jnp.clip(prev_index, 0, slots_all - 1).astype(jnp.int32)
    has_prev = live & ((slot > 0) | (device > 0))
    next_index = jnp.where(slot + 1 < count, flat + 1, (device + 1) * CAP)
    next_index = jnp.clip(next_index, 0, slots_all - 1).astype(jnp.int32)
    has_next = live & ((slot + 1 < count) | (device < N_TRACK - 1))
    livef = live.astype(jnp.float32)
    lower_on = links.astype(jnp.float32) * has_prev.astype(jnp.float32)[None, :]
    upper_on = lower_on[:, next_index] * has_next.astype(jnp.float32)[None, :]

    def operate(vec):
        own = apply_blocks(principal_tiles, vec)
        low = apply_blocks(lower_blocks, vec[:, prev_index]) * lower_on[:, :, None]
        up = apply_transposed(lower_blocks, vec)[:, next_index] * upper_on[:, :, None]
        zero = jnp.zeros((1, slots_all, width), jnp.float32)
        below = jnp.concatenate([zero, vec[:-1]], axis=0)
        cross = apply_blocks(coupling_blocks, below)
        back = apply_transposed(coupling_blocks, vec)
        back = jnp.concatenate([back[1:], zero], axis=0)
        return (own + low + up + cross + back) * livef[None, :, None]

    def sweep_strip(precond, lower, resid, on_row):
        def step(prev, item):
            pmat, lmat, rvec, onv, alive = item
            inner = rvec - onv * jnp.dot(lmat.astype(jnp.float32), prev, precision=lax.Precision.HIGHEST)
            value = jnp.dot(pmat.astype(jnp.float32), inner, precision=lax.Precision.HIGHEST)
            return jnp.where(alive > 0, value, prev), value * alive
        _, values = lax.scan(step, jnp.zeros((width,), jnp.float32), (precond, lower, resid, on_row, livef))
        return values

    def precondition(resid):
        return jax.vmap(sweep_strip)(precond_blocks, lower_blocks, resid, lower_on)

    solution = jnp.zeros_like(rhs)
    residual = rhs * livef[None, :, None]
    for step_number in range(ITERS):
        direction = precondition(residual)
        image = operate(direction)
        alpha = jnp.sum(residual * image) / (jnp.sum(image * image) + 1e-6)
        solution = solution + alpha * direction
        residual = residual - alpha * image
    return solution, residual
```

```python
import functools

import jax
import jax.numpy as jnp
from jax import lax
from jax.experimental import pallas as pl
from jax.experimental.pallas import tpu as pltpu
from jax.sharding import PartitionSpec as P

ITERS = 6
CHAINS = 2
ROWS = 8
NT = (((1,), (1,)), ((), ()))
NN = (((1,), (0,)), ((), ()))
VMEM = pl.BlockSpec(memory_space=pltpu.VMEM)
SMEM = pl.BlockSpec(memory_space=pltpu.SMEM)
F32 = jnp.float32


def pieces(value):
    high = value.astype(jnp.bfloat16).astype(F32)
    rest = value - high
    middle = rest.astype(jnp.bfloat16).astype(F32)
    low = rest - middle
    return high, middle, low


def split_row(row):
    high, middle, low = pieces(row)
    return jnp.concatenate([high, middle, low, jnp.zeros_like(low)], axis=0).astype(jnp.bfloat16)


def times(lhs, matrix, dims):
    out = lax.dot_general(lhs, matrix, dims, preferred_element_type=F32)
    return out[:ROWS] + out[ROWS : 2 * ROWS] + out[2 * ROWS : 3 * ROWS]


def times_matrix(value, matrix, dims):
    high, middle, low = pieces(value)
    lhs = jnp.concatenate([high, middle, low], axis=0).astype(jnp.bfloat16)
    out = lax.dot_general(lhs, matrix, dims, preferred_element_type=F32)
    n = value.shape[0]
    return out[:n] + out[n : 2 * n] + out[2 * n :]


def spread(row):
    return jnp.transpose(jnp.broadcast_to(row, (128, row.shape[1])))


def times_f32(column, matrix):
    wide = jnp.concatenate([column] * (matrix.shape[1] // 128), axis=1)
    return jnp.sum(matrix * wide, axis=0, keepdims=True)


def wide_row(ref, j):
    return jnp.broadcast_to(ref[j : j + 1, :], (ROWS, ref.shape[1]))


def sweep(x_ref, lower_ref, precond_ref, on_ref, live_ref, local_ref, cap):
    length = cap // CHAINS
    state = [None] * CHAINS
    first = None
    for t in range(length):
        for q in range(CHAINS):
            j = q * length + t
            inner = wide_row(x_ref, j)
            if t > 0:
                inner = inner - on_ref[j] * times(split_row(state[q]), lower_ref[j], NT)
            value = times(split_row(inner), precond_ref[j], NT)
            before = state[q] if t > 0 else jnp.zeros_like(value)
            state[q] = jnp.where(live_ref[j] > 0, value, before)
            local_ref[j : j + 1, :] = state[q][:1]
            if j == 0:
                first = on_ref[0] * times(split_row(state[q]), lower_ref[0], NN)
    return state, first


def send_ends(state, first, maps_ref, residual, image, track, n_track, length, out_ref):
    end = state[0][:1]
    for q in range(1, CHAINS):
        end = state[q][:1] + times_f32(spread(end), maps_ref[q * length + length - 1])
    if residual is None:
        dots = [jnp.zeros((1, 128), F32)] * 2
    else:
        dots = []
        for left in (residual, image):
            partial = jnp.sum(left * image, axis=0, keepdims=True)
            dots.append(sum(partial[:, i : i + 128] for i in range(0, partial.shape[1], 128)))
    half = end.shape[1] // 128
    to_later = jnp.concatenate([end[:, 128 * i : 128 * i + 128] for i in range(half)] + dots, axis=0)
    to_earlier = jnp.concatenate(
        [first[:1, 128 * i : 128 * i + 128] for i in range(half)] + dots, axis=0
    )
    for i in range(out_ref.shape[0]):
        out_ref[i] = jnp.where(i % n_track > track, to_later, to_earlier)


def maps_kernel(cap, lower_ref, precond_ref, on_ref, live_ref, maps_ref, total_ref, edge_ref):
    width = lower_ref.shape[-1]
    length = cap // CHAINS
    rows = lax.broadcasted_iota(jnp.int32, (width, width), 0)
    cols = lax.broadcasted_iota(jnp.int32, (width, width), 1)
    ident = jnp.where(rows == cols, 1.0, 0.0).astype(F32)
    state = [ident] * CHAINS
    for t in range(length):
        for q in range(CHAINS):
            j = q * length + t
            if t == 0:
                inner = lax.dot_general(
                    ident.astype(jnp.bfloat16), lower_ref[j], NT, preferred_element_type=F32
                )
                value = lax.dot_general(
                    inner.astype(jnp.bfloat16), precond_ref[j], NT, preferred_element_type=F32
                )
            else:
                inner = times_matrix(state[q], lower_ref[j], NT)
                value = times_matrix(inner, precond_ref[j], NT)
            state[q] = jnp.where(live_ref[j] > 0, -on_ref[j] * value, state[q])
            maps_ref[j] = state[q]
            if j == 0:
                edge_ref[...] = times_matrix(state[q], lower_ref[0], NN)
    total = state[0]
    for q in range(1, CHAINS):
        total = jnp.dot(total, state[q], precision=lax.Precision.HIGHEST)
    total_ref[...] = total


def entry_kernel(n_track, pos_ref, totals_ref, out_ref):
    track = pos_ref[0]
    value = None
    for i in range(1, n_track - 1):
        index = jnp.bitwise_xor(jnp.maximum(track - i, 0), track)
        nearer = totals_ref[index]
        value = nearer if value is None else jnp.dot(nearer, value, precision=lax.Precision.HIGHEST)
        out_ref[i - 1] = value


def start_kernel(cap, n_track, rhs_ref, lower_ref, precond_ref, maps_ref, on_ref, live_ref, pos_ref, local_ref, send_ref):
    state, first = sweep(rhs_ref, lower_ref, precond_ref, on_ref, live_ref, local_ref, cap)
    send_ends(state, first, maps_ref, None, None, pos_ref[0], n_track, cap // CHAINS, send_ref)


def direction_kernel(
    cap, n_track, recv_ref, local_ref, maps_ref, entry_ref, edge_map_ref, coupling_ref, live_ref, pos_ref,
    value_ref, first_ref, second_ref, rims_ref,
):
    track, strip = pos_ref[0], pos_ref[1]
    width = local_ref.shape[1]
    length = cap // CHAINS
    half = width // 128
    base = strip * n_track

    def end_of(i):
        got = recv_ref[base + jnp.maximum(track - i, 0)]
        got = jnp.where(track - i >= 0, got, 0.0)
        return [got[h : h + 1] for h in range(half)]

    entry = jnp.concatenate(end_of(1), axis=1)
    for i in range(2, n_track):
        column = jnp.concatenate([spread(part) for part in end_of(i)], axis=0)
        entry = entry + times_f32(column, entry_ref[i - 2])
    rims_ref[0:1, :] = entry
    columns = [spread(entry)]
    for q in range(1, CHAINS):
        last = q * length - 1
        begin = local_ref[last : last + 1, :] + times_f32(columns[-1], maps_ref[last])
        columns.append(spread(begin))
    even = strip % 2 == 0
    for j in range(cap):
        value = local_ref[j : j + 1, :] + times_f32(columns[j // length], maps_ref[j])
        masked = jnp.where(live_ref[j] > 0, value, 0.0)
        value_ref[j : j + 1, :] = masked
        crossed = times(split_row(jnp.broadcast_to(masked, (ROWS, width))), coupling_ref[j], NN)[:1]
        first_ref[j : j + 1, :] = jnp.where(even, masked, crossed)
        second_ref[j : j + 1, :] = jnp.where(even, crossed, masked)
    ahead = recv_ref[base + jnp.minimum(track + 1, n_track - 1)]
    ahead = jnp.concatenate([ahead[h : h + 1] for h in range(half)], axis=1)
    ahead = ahead + times_f32(spread(value), edge_map_ref[...])
    rims_ref[1:2, :] = jnp.where(track < n_track - 1, ahead, 0.0)


def local_kernel(cap, value_ref, rims_ref, diag_ref, lower_ref, on_ref, pos_ref, base_ref):
    count = pos_ref[2]
    lowered = on_ref[0] * times(split_row(wide_row(rims_ref, 0)), lower_ref[0], NT)
    edge = wide_row(rims_ref, 1)
    held = None
    for j in range(cap):
        lhs = split_row(wide_row(value_ref, j))
        own = times(lhs, diag_ref[j], NT) + lowered
        if j > 0:
            held = held + on_ref[j] * times(lhs, lower_ref[j], NN)
            base_ref[j - 1 : j, :] = held[:1]
        if j < cap - 1:
            lowered = on_ref[j + 1] * times(lhs, lower_ref[j + 1], NT)
        held = own + jnp.where(count - 1 == j, edge, 0.0)
    base_ref[cap - 1 : cap, :] = held[:1]


def alpha_of(recv_ref, half):
    total = jnp.sum(recv_ref[...], axis=0)
    inner = jnp.sum(total[half : half + 1], axis=1, keepdims=True)
    energy = jnp.sum(total[half + 1 : half + 2], axis=1, keepdims=True)
    return inner / (energy + 1e-6)


def update_kernel(
    cap, n_track, first, last, base_ref, first_ref, second_ref, recv_ref, value_ref, state_ref, mask_ref,
    coupling_ref, lower_ref, precond_ref, maps_ref, on_ref, live_ref, pos_ref, next_ref, local_ref, send_ref,
):
    track, strip = pos_ref[0], pos_ref[1]
    width = base_ref.shape[1]
    odd = strip % 2 == 1
    image_ref = next_ref.at[1]
    one, two = first_ref[...], second_ref[...]
    below = jnp.where(odd, one, two)
    above = jnp.where(odd, two, one)
    image_ref[...] = base_ref[...] + above
    for j in range(cap):
        row = jnp.broadcast_to(below[j : j + 1, :], (ROWS, width))
        crossed = times(split_row(row), coupling_ref[j], NT)
        image_ref[j : j + 1, :] = image_ref[j : j + 1, :] + crossed[:1]
    image = image_ref[...] * mask_ref[...]
    if first:
        next_ref[0] = state_ref[0]
        next_ref[2] = value_ref[...]
        next_ref[3] = jnp.zeros_like(image)
        next_ref[1] = image
    else:
        alpha = alpha_of(recv_ref, width // 128)
        next_ref[0] = state_ref[0] - alpha * state_ref[1]
        next_ref[3] = state_ref[3] + alpha * state_ref[2]
        next_ref[2] = state_ref[2] - alpha * value_ref[...]
        next_ref[1] = state_ref[1] - alpha * image
    residual, image = next_ref[0], next_ref[1]
    if last:
        state, edge = [jnp.zeros((1, width), F32)], jnp.zeros((1, width), F32)
        local_ref[...] = jnp.zeros_like(image)
        dots = []
        for left in (residual, image):
            partial = jnp.sum(left * image, axis=0, keepdims=True)
            dots.append(sum(partial[:, i : i + 128] for i in range(0, width, 128)))
        packed = jnp.concatenate([jnp.zeros((width // 128, 128), F32)] + dots, axis=0)
        for i in range(send_ref.shape[0]):
            send_ref[i] = packed
    else:
        state, edge = sweep(image_ref, lower_ref, precond_ref, on_ref, live_ref, local_ref, cap)
        send_ends(state, edge, maps_ref, residual, image, track, n_track, cap // CHAINS, send_ref)


def final_kernel(recv_ref, state_ref, solution_ref, residual_ref):
    alpha = alpha_of(recv_ref, state_ref.shape[2] // 128)
    solution_ref[...] = state_ref[3] + alpha * state_ref[2]
    residual_ref[...] = state_ref[0] - alpha * state_ref[1]


def call(kernel, outs, specs, *args):
    return pl.pallas_call(
        kernel,
        out_shape=[jax.ShapeDtypeStruct(shape, F32) for shape in outs],
        in_specs=specs,
        out_specs=[VMEM] * len(outs),
        compiler_params=pltpu.CompilerParams(vmem_limit_bytes=40 * 1024 * 1024),
    )(*args)


def body(rhs, principal_tiles, lower_blocks, coupling_blocks, precond_blocks, seg_blocks, links):
    cap, width = rhs.shape[1:]
    n_track, n_strip = lax.axis_size("track"), lax.axis_size("strip")
    track, strip = lax.axis_index("track"), lax.axis_index("strip")
    count = seg_blocks[0]
    slots = jnp.arange(cap, dtype=jnp.int32)
    live = (slots < count).astype(F32)
    on = links[0].astype(F32) * live * jnp.where((slots > 0) | (track > 0), 1.0, 0.0)
    mask = jnp.broadcast_to(live[:, None], (cap, width))
    pos = jnp.stack([track, strip, count]).astype(jnp.int32)
    diag, lower, coupling, precond = (
        principal_tiles[0], lower_blocks[0], coupling_blocks[0], precond_blocks[0],
    )
    whole = n_track * n_strip
    block = (cap, width)
    chunk = (whole, width // 128 + 2, 128)

    maps, total, edge_map = call(
        functools.partial(maps_kernel, cap),
        [(cap, width, width), (width, width), (width, width)],
        [VMEM, VMEM, SMEM, SMEM],
        lower, precond, on, live,
    )
    gathered = [total]
    for m in range(2, n_track, 2):
        gathered.append(lax.ppermute(total, "track", [(i, i ^ m) for i in range(n_track)]))
    gathered = jnp.stack(gathered)
    other = lax.ppermute(gathered, "track", [(i, i ^ 1) for i in range(n_track)])
    totals = jnp.stack([gathered, other], axis=1).reshape(n_track, width, width)
    edge_map = lax.ppermute(edge_map, "track", [(i + 1, i) for i in range(n_track - 1)])
    entries, = call(
        functools.partial(entry_kernel, n_track),
        [(n_track - 2, width, width)],
        [SMEM, VMEM],
        pos, totals,
    )

    residual = rhs[0] * mask
    local, send = call(
        functools.partial(start_kernel, cap, n_track),
        [block, chunk],
        [VMEM] * 4 + [SMEM] * 3,
        residual, lower, precond, maps, on, live, pos,
    )
    state = jnp.broadcast_to(residual[None], (4,) + block)
    pairs = [(i, i ^ 1) for i in range(n_strip) if i ^ 1 < n_strip]
    cross = [(i, j) for k in range(1, n_strip - 1, 2) for i, j in ((k, k + 1), (k + 1, k))]
    for step_number in range(ITERS):
        recv = lax.all_to_all(send, ("strip", "track"), 0, 0)
        value, first, second, rims = call(
            functools.partial(direction_kernel, cap, n_track),
            [block, block, block, (2, width)],
            [VMEM] * 6 + [SMEM] * 2,
            recv, local, maps, entries, edge_map, coupling, live, pos,
        )
        first = lax.ppermute(first, "strip", pairs)
        second = lax.ppermute(second, "strip", cross)
        base, = call(
            functools.partial(local_kernel, cap),
            [block],
            [VMEM] * 4 + [SMEM] * 2,
            value, rims, diag, lower, on, pos,
        )
        state, local, send = call(
            functools.partial(update_kernel, cap, n_track, step_number == 0, step_number == ITERS - 1),
            [(4,) + block, block, chunk],
            [VMEM] * 11 + [SMEM] * 3,
            base, first, second, recv, value, state, mask, coupling, lower, precond, maps, on, live, pos,
        )
    recv = lax.all_to_all(send, ("strip", "track"), 0, 0)
    solution, residual = call(final_kernel, [block, block], [VMEM] * 2, recv, state)
    return (solution[None], residual[None])


def solution(mesh):
    in_specs = (
        P("strip", "track", None),
        P("strip", "track", None, None),
        P("strip", "track", None, None),
        P("strip", "track", None, None),
        P("strip", "track", None, None),
        P("track"),
        P("strip", "track"),
    )
    out_specs = (P("strip", "track", None), P("strip", "track", None))
    return jax.shard_map(body, mesh=mesh, in_specs=in_specs, out_specs=out_specs, check_vma=False)
```

```python
import functools
import math

import jax
import jax.numpy as jnp
from jax import lax
from jax.experimental import pallas as pl
from jax.experimental.pallas import tpu as pltpu
from jax.sharding import PartitionSpec as P

ITERS = 6
CHAINS = 4
ROWS = 8
EARLY = 2
VMEM_BYTES = 16 * 1024 * 1024
PINNED = 1 << 19
NT = (((1,), (1,)), ((), ()))
NN = (((1,), (0,)), ((), ()))
VMEM = pl.BlockSpec(memory_space=pltpu.VMEM)
HBM = pl.BlockSpec(memory_space=pltpu.MemorySpace.HBM)
SMEM = pl.BlockSpec(memory_space=pltpu.SMEM)
F32 = jnp.float32


def pieces(value):
    high = value.astype(jnp.bfloat16)
    rest = value - high.astype(F32)
    middle = rest.astype(jnp.bfloat16)
    low = (rest - middle.astype(F32)).astype(jnp.bfloat16)
    return jnp.concatenate([high, middle, low], axis=0)


def split_row(row):
    return pieces(jnp.concatenate([row, row], axis=0))


def times(lhs, matrix, dims):
    out = lax.dot_general(lhs, matrix, dims, preferred_element_type=F32)
    return out[:ROWS] + out[2 * ROWS : 3 * ROWS] + out[4 * ROWS : 5 * ROWS]


def times_matrix(value, matrix, dims):
    out = lax.dot_general(pieces(value), matrix, dims, preferred_element_type=F32)
    n = value.shape[0]
    return out[:n] + out[n : 2 * n] + out[2 * n :]


def spread(row):
    return jnp.transpose(jnp.broadcast_to(row, (128, row.shape[1])))


def times_f32(column, matrix):
    wide = jnp.concatenate([column] * (matrix.shape[1] // 128), axis=1)
    return jnp.sum(matrix * wide, axis=0, keepdims=True)


def wide_row(ref, j):
    return jnp.broadcast_to(ref[j : j + 1, :], (ROWS, ref.shape[1]))


def is_live(pos_ref, j):
    return j < pos_ref[2]


def link(links_ref, pos_ref, j):
    joined = links_ref[0, j] if j else jnp.where(pos_ref[0] > 0, links_ref[0, 0], 0)
    return jnp.where(is_live(pos_ref, j), joined, 0).astype(F32)


def live_mask(pos_ref, shape):
    return lax.broadcasted_iota(jnp.int32, shape, 0) < pos_ref[2]


def dot_parts(residual, image):
    parts = []
    for left in (residual, image):
        partial = jnp.sum(left * image, axis=0, keepdims=True)
        parts.append(sum(partial[:, i : i + 128] for i in range(0, partial.shape[1], 128)))
    return parts


def halves(row):
    return [row[:, i : i + 128] for i in range(0, row.shape[1], 128)]


def send_ends(end, first, dots, other_ref, pos_ref, n_track, out_ref):
    track = pos_ref[0]
    carried = jnp.where(track % 2 == 0, times_f32(spread(end), other_ref[...]), end)
    near = jnp.concatenate(halves(end) + dots, axis=0)
    far = jnp.concatenate(halves(carried) + dots, axis=0)
    back = jnp.concatenate(halves(first) + dots, axis=0)
    for i in range(out_ref.shape[0]):
        ahead = i % n_track - track
        out_ref[i] = jnp.where(ahead > 1, far, jnp.where(ahead == 1, near, back))


def chain_end(state, maps_ref, length):
    end = state[0][:1]
    for q in range(1, CHAINS):
        end = state[q][:1] + times_f32(spread(end), maps_ref[q * length + length - 1])
    return end


def maps_kernel(
    cap, rhs_hbm, lower_hbm, precond_hbm, diag_hbm, coupling_hbm, links_ref, pos_ref,
    maps_ref, total_ref, edge_ref, local_ref, ends_ref, lower_ref, precond_ref, diag_ref, coupling_ref,
    rhs_ref, sems,
):
    width = lower_ref.shape[-1]
    length = cap // CHAINS
    copies = [pltpu.make_async_copy(rhs_hbm, rhs_ref, sems.at[0])]

    def load(source, target, start, count):
        rows = pl.ds(start, count)
        copies.append(pltpu.make_async_copy(source.at[rows], target.at[rows], sems.at[len(copies)]))

    for begin, end in ((0, EARLY), (EARLY, length)):
        for source, target in ((lower_hbm, lower_ref), (precond_hbm, precond_ref)):
            for q in range(CHAINS):
                load(source, target, q * length + begin, end - begin)
    load(diag_hbm, diag_ref, 0, cap)
    load(coupling_hbm, coupling_ref, 0, cap)
    for copy in copies:
        copy.start()
    early = 1 + 2 * CHAINS
    for copy in copies[:early]:
        copy.wait()
    rows = lax.broadcasted_iota(jnp.int32, (width, width), 0)
    cols = lax.broadcasted_iota(jnp.int32, (width, width), 1)
    ident = jnp.where(rows == cols, 1.0, 0.0).astype(F32)
    state = [ident] * CHAINS
    local = [None] * CHAINS
    for t in range(length):
        if t == EARLY:
            for copy in copies[early:-2]:
                copy.wait()
        for q in range(CHAINS):
            j = q * length + t
            live, on = is_live(pos_ref, j), link(links_ref, pos_ref, j)
            if t == 0:
                inner = lax.dot_general(
                    ident.astype(jnp.bfloat16), lower_ref[j], NT, preferred_element_type=F32
                )
                value = lax.dot_general(
                    inner.astype(jnp.bfloat16), precond_ref[j], NT, preferred_element_type=F32
                )
            else:
                inner = times_matrix(state[q], lower_ref[j], NT)
                value = times_matrix(inner, precond_ref[j], NT)
            state[q] = jnp.where(live, -on * value, state[q])
            maps_ref[j] = state[q]
            inner = wide_row(rhs_ref, j)
            if t > 0:
                inner = inner - on * times(split_row(local[q]), lower_ref[j], NT)
            value = times(split_row(inner), precond_ref[j], NT)
            local[q] = jnp.where(live, value, local[q] if t > 0 else 0.0)
            local_ref[j : j + 1, :] = local[q][:1]
            if j == 0:
                edge_ref[...] = times_matrix(state[q], lower_ref[0], NN)
                ends_ref[1:2, :] = (on * times(split_row(local[q]), lower_ref[0], NN))[:1]
    while len(state) > 1:
        pairs = zip(state[::2], state[1::2])
        state = [jnp.dot(a, b, precision=lax.Precision.HIGHEST) for a, b in pairs]
    total_ref[...] = state[0]
    ends_ref[0:1, :] = chain_end(local, maps_ref, length)
    for copy in copies[-2:]:
        copy.wait()


def pair_kernel(n_track, total_ref, other_ref, ends_ref, pos_ref, *refs):
    chip_ref, send_ref = refs[-2:]
    first_core = pos_ref[0] % 2 == 0
    own, other = total_ref[...], other_ref[...]
    half = own.shape[0] // 2
    early = jnp.where(first_core, own[:half], other[half:])
    late = jnp.where(first_core, other, own)
    chip_ref[...] = jnp.dot(early, late, precision=lax.Precision.HIGHEST)
    dots = [jnp.zeros((1, 128), F32)] * 2
    send_ends(ends_ref[0:1, :], ends_ref[1:2, :], dots, other_ref, pos_ref, n_track, send_ref)


def direction_kernel(cap, n_track, recv_ref, local_ref, maps_ref, other_ref, coupling_ref, *refs):
    chip_refs, (pos_ref, value_ref, first_ref, second_ref, entry_ref) = refs[:-5], refs[-5:]
    track, strip = pos_ref[0], pos_ref[1]
    width = local_ref.shape[1]
    length = cap // CHAINS
    half = width // 128
    base = strip * n_track
    chip = track // 2

    def chunk(index, valid):
        got = recv_ref[base + jnp.clip(index, 0, n_track - 1)]
        got = jnp.where(valid, got, 0.0)
        return jnp.concatenate([got[h : h + 1] for h in range(half)], axis=1)

    def chip_end(i):
        valid = chip - i >= 0
        return chunk(2 * (chip - i), valid) + chunk(2 * (chip - i) + 1, valid)

    def chip_map(i):
        mine, paired = chip_refs[i][...], chip_refs[i + len(chip_refs) // 2][...]
        first_core = track % 2 == 0
        top, bottom = jnp.where(first_core, mine, paired), jnp.where(first_core, paired, mine)
        return jnp.concatenate([top, bottom], axis=0)

    furthest = n_track // 2 - 1
    entry = chip_end(furthest)
    for i in range(furthest - 1, 0, -1):
        entry = chip_end(i) + times_f32(spread(entry), chip_map(i - 1))
    inside = chunk(track - 1, track > 0) + times_f32(spread(entry), other_ref[...])
    entry = jnp.where(track % 2 == 1, inside, entry)
    entry_ref[...] = entry
    columns = [spread(entry)]
    for q in range(1, CHAINS):
        last = q * length - 1
        begin = local_ref[last : last + 1, :] + times_f32(columns[-1], maps_ref[last])
        columns.append(spread(begin))
    even = strip % 2 == 0
    for j in range(cap):
        value = local_ref[j : j + 1, :] + times_f32(columns[j // length], maps_ref[j])
        masked = jnp.where(is_live(pos_ref, j), value, 0.0)
        value_ref[j : j + 1, :] = masked
        crossed = times(split_row(jnp.broadcast_to(masked, (ROWS, width))), coupling_ref[j], NN)[:1]
        first_ref[j : j + 1, :] = jnp.where(even, masked, crossed)
        second_ref[j : j + 1, :] = jnp.where(even, crossed, masked)


def local_kernel(cap, value_ref, entry_ref, diag_ref, lower_ref, links_ref, pos_ref, base_ref):
    lowered = link(links_ref, pos_ref, 0) * times(split_row(wide_row(entry_ref, 0)), lower_ref[0], NT)
    held = None
    for j in range(cap):
        lhs = split_row(wide_row(value_ref, j))
        own = times(lhs, diag_ref[j], NT) + lowered
        if j > 0:
            held = held + link(links_ref, pos_ref, j) * times(lhs, lower_ref[j], NN)
            base_ref[j - 1 : j, :] = held[:1]
        if j < cap - 1:
            lowered = link(links_ref, pos_ref, j + 1) * times(lhs, lower_ref[j + 1], NT)
        held = own
    base_ref[cap - 1 : cap, :] = held[:1]


def alpha_of(recv_ref, half):
    total = jnp.sum(recv_ref[...], axis=0)
    inner = jnp.sum(total[half : half + 1], axis=1, keepdims=True)
    energy = jnp.sum(total[half + 1 : half + 2], axis=1, keepdims=True)
    return inner / (energy + 1e-6)


def update_kernel(
    cap, n_track, first, base_ref, first_ref, second_ref, recv_ref, value_ref, state_ref, edge_map_ref, coupling_ref,
    lower_ref, precond_ref, maps_ref, other_ref, links_ref, pos_ref, next_ref, local_ref, send_ref,
):
    track, strip, count = pos_ref[0], pos_ref[1], pos_ref[2]
    width = base_ref.shape[1]
    length = cap // CHAINS
    odd = strip % 2 == 1
    image_ref = next_ref.at[1]
    one, two = first_ref[...], second_ref[...]
    below = jnp.where(odd, one, two)
    above = jnp.where(odd, two, one)
    ahead = recv_ref[strip * n_track + jnp.minimum(track + 1, n_track - 1)]
    ahead = jnp.concatenate([ahead[h : h + 1] for h in range(width // 128)], axis=1)
    ahead = ahead + times_f32(spread(value_ref[pl.ds(count - 1, 1), :]), edge_map_ref[...])
    ahead = jnp.where(track < n_track - 1, ahead, 0.0)
    at_end = lax.broadcasted_iota(jnp.int32, (cap, width), 0) == count - 1
    image_ref[...] = base_ref[...] + above + jnp.where(at_end, ahead, 0.0)
    for j in range(cap):
        row = jnp.broadcast_to(below[j : j + 1, :], (ROWS, width))
        crossed = times(split_row(row), coupling_ref[j], NT)
        image_ref[j : j + 1, :] = image_ref[j : j + 1, :] + crossed[:1]
    mask = live_mask(pos_ref, (cap, width))
    image = jnp.where(mask, image_ref[...], 0.0)
    if first:
        next_ref[0] = jnp.where(mask, state_ref[...], 0.0)
        next_ref[2] = value_ref[...]
        next_ref[3] = jnp.zeros_like(image)
        next_ref[1] = image
    else:
        alpha = alpha_of(recv_ref, width // 128)
        next_ref[0] = state_ref[0] - alpha * state_ref[1]
        next_ref[3] = state_ref[3] + alpha * state_ref[2]
        next_ref[2] = state_ref[2] - alpha * value_ref[...]
        next_ref[1] = state_ref[1] - alpha * image
    dots = dot_parts(next_ref[0], next_ref[1])
    if local_ref is None:
        packed = jnp.concatenate([jnp.zeros((width // 128, 128), F32)] + dots, axis=0)
        for i in range(send_ref.shape[0]):
            send_ref[i] = packed
        return
    state = [None] * CHAINS
    for t in range(length):
        for q in range(CHAINS):
            j = q * length + t
            inner = wide_row(image_ref, j)
            if t > 0:
                lowered = times(split_row(state[q]), lower_ref[j], NT)
                inner = inner - link(links_ref, pos_ref, j) * lowered
            value = times(split_row(inner), precond_ref[j], NT)
            state[q] = jnp.where(is_live(pos_ref, j), value, state[q] if t > 0 else 0.0)
            local_ref[j : j + 1, :] = state[q][:1]
            if j == 0:
                edge = link(links_ref, pos_ref, 0) * times(split_row(state[q]), lower_ref[0], NN)
    send_ends(chain_end(state, maps_ref, length), edge[:1], dots, other_ref, pos_ref, n_track, send_ref)


def last_update_kernel(cap, n_track, *refs):
    update_kernel(cap, n_track, False, *refs[:-1], None, refs[-1])


def final_kernel(recv_ref, state_ref, solution_ref, residual_ref):
    alpha = alpha_of(recv_ref, state_ref.shape[2] // 128)
    solution_ref[...] = state_ref[3] + alpha * state_ref[2]
    residual_ref[...] = state_ref[0] - alpha * state_ref[1]


def call(kernel, outs, specs, *args, scratch=(), vmem=VMEM_BYTES):
    outs = [out if len(out) == 2 and isinstance(out[0], tuple) else (out, F32) for out in outs]
    args = [
        pltpu.with_memory_space_constraint(arg, spec.memory_space) if arg.size >= PINNED or spec is HBM else arg
        for arg, spec in zip(args, specs)
    ]
    return pl.pallas_call(
        kernel,
        out_shape=[
            pltpu.VMEM(shape, dtype) if math.prod(shape) >= PINNED else jax.ShapeDtypeStruct(shape, dtype)
            for shape, dtype in outs
        ],
        in_specs=specs,
        out_specs=[VMEM] * len(outs),
        scratch_shapes=scratch,
        compiler_params=pltpu.CompilerParams(vmem_limit_bytes=vmem),
    )(*args)


def body(rhs, principal_tiles, lower_blocks, coupling_blocks, precond_blocks, seg_blocks, links):
    cap, width = rhs.shape[1:]
    n_track, n_strip = lax.axis_size("track"), lax.axis_size("strip")
    track, strip = lax.axis_index("track"), lax.axis_index("strip")
    pos = jnp.stack([track, strip, seg_blocks[0]]).astype(jnp.int32)
    rhs = rhs[0]
    whole = n_track * n_strip
    chips = n_track // 2
    block = (cap, width)
    square = (width, width)
    stack = (cap, width, width)
    chunk = (whole, width // 128 + 2, 128)
    swap = [(i, i ^ 1) for i in range(n_track)]

    maps, total, edge_map, local, ends, lower, precond, diag, coupling = call(
        functools.partial(maps_kernel, cap),
        [stack, square, square, block, (2, width)] + [(stack, jnp.bfloat16)] * 4,
        [HBM] * 5 + [SMEM] * 2,
        rhs, lower_blocks[0], precond_blocks[0], principal_tiles[0], coupling_blocks[0], links, pos,
        scratch=[pltpu.VMEM(block, F32), pltpu.SemaphoreType.DMA((4 * CHAINS + 3,))],
    )
    other = lax.ppermute(total, "track", swap)
    chip, send = call(
        functools.partial(pair_kernel, n_track),
        [(width // 2, width), chunk],
        [VMEM] * 3 + [SMEM] + [VMEM] * 5,
        total, other, ends, pos, maps, lower, precond, diag, coupling,
    )
    nearer = [
        lax.ppermute(chip, "track", [(i, i + 2 * k) for i in range(2, n_track - 2 * k)])
        for k in range(1, chips - 1)
    ]
    state = rhs
    pairs = [(i, i ^ 1) for i in range(n_strip) if i ^ 1 < n_strip]
    cross = [(i, j) for k in range(1, n_strip - 1, 2) for i, j in ((k, k + 1), (k + 1, k))]
    for step_number in range(ITERS):
        recv = lax.all_to_all(send, ("strip", "track"), 0, 0)
        if step_number == 0:
            recv, *nearer = lax.optimization_barrier((recv, *nearer))
            nearer += [lax.ppermute(part, "track", swap) for part in nearer]
        value, first, second, entry = call(
            functools.partial(direction_kernel, cap, n_track),
            [block, block, block, (1, width)],
            [VMEM] * (5 + len(nearer)) + [SMEM],
            recv, local, maps, other, coupling, *nearer, pos,
        )
        if step_number == 0:
            edge_map, entry = lax.optimization_barrier((edge_map, entry))
            edge_map = lax.ppermute(edge_map, "track", [(i + 1, i) for i in range(n_track - 1)])
        first = lax.ppermute(first, "strip", pairs)
        second = lax.ppermute(second, "strip", cross)
        base, = call(
            functools.partial(local_kernel, cap),
            [block],
            [VMEM] * 4 + [SMEM] * 2,
            value, entry, diag, lower, links, pos,
        )
        args = (base, first, second, recv, value, state, edge_map, coupling, lower, precond, maps, other, links, pos)
        specs = [VMEM] * 12 + [SMEM] * 2
        if step_number < ITERS - 1:
            kernel = functools.partial(update_kernel, cap, n_track, step_number == 0)
            state, local, send = call(kernel, [(4,) + block, block, chunk], specs, *args)
        else:
            kernel = functools.partial(last_update_kernel, cap, n_track)
            state, send = call(kernel, [(4,) + block, chunk], specs, *args)
    recv = lax.all_to_all(send, ("strip", "track"), 0, 0)
    solution, residual = call(final_kernel, [block, block], [VMEM] * 2, recv, state)
    return (solution[None], residual[None])


def solution(mesh):
    in_specs = (
        P("strip", "track", None),
        P("strip", "track", None, None),
        P("strip", "track", None, None),
        P("strip", "track", None, None),
        P("strip", "track", None, None),
        P("track"),
        P("strip", "track"),
    )
    out_specs = (P("strip", "track", None), P("strip", "track", None))
    return jax.shard_map(body, mesh=mesh, in_specs=in_specs, out_specs=out_specs, check_vma=False)
```

```python
import functools
import math

import jax
import jax.numpy as jnp
from jax import lax
from jax.experimental import pallas as pl
from jax.experimental.pallas import tpu as pltpu
from jax.sharding import PartitionSpec as P

ITERS = 6
CHAINS = 4
ROWS = 8
EARLY = 1
VMEM_BYTES = 16 * 1024 * 1024
PINNED = 1 << 19
NT = (((1,), (1,)), ((), ()))
NN = (((1,), (0,)), ((), ()))
VMEM = pl.BlockSpec(memory_space=pltpu.VMEM)
HBM = pl.BlockSpec(memory_space=pltpu.MemorySpace.HBM)
SMEM = pl.BlockSpec(memory_space=pltpu.SMEM)
F32 = jnp.float32


def pieces(value):
    high = value.astype(jnp.bfloat16)
    rest = value - high.astype(F32)
    middle = rest.astype(jnp.bfloat16)
    low = (rest - middle.astype(F32)).astype(jnp.bfloat16)
    return jnp.concatenate([high, middle, low], axis=0)


def split_row(row):
    return pieces(jnp.concatenate([row, row], axis=0))


def times(lhs, matrix, dims):
    out = lax.dot_general(lhs, matrix, dims, preferred_element_type=F32)
    return out[:ROWS] + out[2 * ROWS : 3 * ROWS] + out[4 * ROWS : 5 * ROWS]


def times_matrix(value, matrix, dims):
    out = lax.dot_general(pieces(value), matrix, dims, preferred_element_type=F32)
    n = value.shape[0]
    return out[:n] + out[n : 2 * n] + out[2 * n :]


def spread(row):
    return jnp.transpose(jnp.broadcast_to(row, (128, row.shape[1])))


def times_f32(column, matrix):
    wide = jnp.concatenate([column] * (matrix.shape[1] // 128), axis=1)
    return jnp.sum(matrix * wide, axis=0, keepdims=True)


def wide_row(ref, j):
    return jnp.broadcast_to(ref[j : j + 1, :], (ROWS, ref.shape[1]))


def is_live(pos_ref, j):
    return j < pos_ref[2]


def link(links_ref, pos_ref, j):
    joined = links_ref[0, j] if j else jnp.where(pos_ref[0] > 0, links_ref[0, 0], 0)
    return jnp.where(is_live(pos_ref, j), joined, 0).astype(F32)


def live_mask(pos_ref, shape):
    return lax.broadcasted_iota(jnp.int32, shape, 0) < pos_ref[2]


def dot_parts(residual, image):
    parts = []
    for left in (residual, image):
        partial = jnp.sum(left * image, axis=0, keepdims=True)
        parts.append(sum(partial[:, i : i + 128] for i in range(0, partial.shape[1], 128)))
    return parts


def halves(row):
    return [row[:, i : i + 128] for i in range(0, row.shape[1], 128)]


def send_ends(end, first, dots, other_ref, pos_ref, n_track, out_ref):
    track = pos_ref[0]
    carried = jnp.where(track % 2 == 0, times_f32(spread(end), other_ref[...]), end)
    near = jnp.concatenate(halves(end) + dots, axis=0)
    far = jnp.concatenate(halves(carried) + dots, axis=0)
    back = jnp.concatenate(halves(first) + dots, axis=0)
    for i in range(out_ref.shape[0]):
        ahead = i % n_track - track
        out_ref[i] = jnp.where(ahead > 1, far, jnp.where(ahead == 1, near, back))


def chain_ends(state, maps_ref, length):
    ends = [state[0][:1]]
    for q in range(1, CHAINS):
        ends.append(state[q][:1] + times_f32(spread(ends[-1]), maps_ref[q * length + length - 1]))
    return ends


def maps_kernel(
    cap, rhs_hbm, links_hbm, lower_hbm, precond_hbm, diag_hbm, coupling_hbm, pos_ref,
    maps_ref, total_ref, edge_ref, local_ref, ends_ref, begins_ref, through_ref,
    lower_ref, precond_ref, diag_ref, coupling_ref,
    rhs_ref, links_ref, sems,
):
    width = lower_ref.shape[-1]
    length = cap // CHAINS
    copies = [
        pltpu.make_async_copy(rhs_hbm, rhs_ref, sems.at[0]),
        pltpu.make_async_copy(links_hbm, links_ref, sems.at[1]),
    ]

    def load(source, target, start, count):
        rows = pl.ds(start, count)
        copies.append(pltpu.make_async_copy(source.at[rows], target.at[rows], sems.at[len(copies)]))

    for begin, end in ((0, EARLY), (EARLY, length)):
        for source, target in ((lower_hbm, lower_ref), (precond_hbm, precond_ref)):
            for q in range(CHAINS):
                load(source, target, q * length + begin, end - begin)
    load(diag_hbm, diag_ref, 0, cap)
    load(coupling_hbm, coupling_ref, 0, cap)
    for copy in copies:
        copy.start()
    early = 2 + 2 * CHAINS
    for copy in copies[:early]:
        copy.wait()
    rows = lax.broadcasted_iota(jnp.int32, (width, width), 0)
    cols = lax.broadcasted_iota(jnp.int32, (width, width), 1)
    ident = jnp.where(rows == cols, 1.0, 0.0).astype(F32)
    state = [ident] * CHAINS
    local = [None] * CHAINS
    for t in range(length):
        if t == EARLY:
            for copy in copies[early:-2]:
                copy.wait()
        for q in range(CHAINS):
            j = q * length + t
            live, on = is_live(pos_ref, j), link(links_ref, pos_ref, j)
            if t == 0:
                inner = lax.dot_general(
                    ident.astype(jnp.bfloat16), lower_ref[j], NT, preferred_element_type=F32
                )
                value = lax.dot_general(
                    inner.astype(jnp.bfloat16), precond_ref[j], NT, preferred_element_type=F32
                )
            else:
                inner = times_matrix(state[q], lower_ref[j], NT)
                value = times_matrix(inner, precond_ref[j], NT)
            state[q] = jnp.where(live, -on * value, state[q])
            maps_ref[j] = state[q]
            inner = wide_row(rhs_ref, j)
            if t > 0:
                inner = inner - on * times(split_row(local[q]), lower_ref[j], NT)
            value = times(split_row(inner), precond_ref[j], NT)
            local[q] = jnp.where(live, value, local[q] if t > 0 else 0.0)
            local_ref[j : j + 1, :] = local[q][:1]
            if j == 0:
                edge_ref[...] = times_matrix(state[q], lower_ref[0], NN)
                ends_ref[1:2, :] = (on * times(split_row(local[q]), lower_ref[0], NN))[:1]
    span = 1
    while span < CHAINS:
        state = [
            state[q] if q < span else jnp.dot(state[q - span], state[q], precision=lax.Precision.HIGHEST)
            for q in range(CHAINS)
        ]
        span *= 2
    for q in range(CHAINS - 1):
        through_ref[q] = state[q]
    total_ref[...] = state[-1]
    ends = chain_ends(local, maps_ref, length)
    ends_ref[0:1, :] = ends[-1]
    begins_ref[...] = jnp.concatenate(ends, axis=0)
    for copy in copies[-2:]:
        copy.wait()


def pair_kernel(n_track, total_ref, other_ref, ends_ref, pos_ref, *refs):
    chip_ref, send_ref = refs[-2:]
    first_core = pos_ref[0] % 2 == 0
    own, other = total_ref[...], other_ref[...]
    half = own.shape[0] // 2
    early = jnp.where(first_core, own[:half], other[half:])
    late = jnp.where(first_core, other, own)
    chip_ref[...] = jnp.dot(early, late, precision=lax.Precision.HIGHEST)
    dots = [jnp.zeros((1, 128), F32)] * 2
    send_ends(ends_ref[0:1, :], ends_ref[1:2, :], dots, other_ref, pos_ref, n_track, send_ref)


def direction_kernel(cap, n_track, recv_ref, local_ref, begins_ref, maps_ref, through_ref, other_ref, coupling_ref, *refs):
    chip_refs, (pos_ref, value_ref, first_ref, second_ref, entry_ref) = refs[:-5], refs[-5:]
    track, strip = pos_ref[0], pos_ref[1]
    width = local_ref.shape[1]
    length = cap // CHAINS
    half = width // 128
    base = strip * n_track
    chip = track // 2

    def chunk(index, valid):
        got = recv_ref[base + jnp.clip(index, 0, n_track - 1)]
        got = jnp.where(valid, got, 0.0)
        return jnp.concatenate([got[h : h + 1] for h in range(half)], axis=1)

    def chip_end(i):
        valid = chip - i >= 0
        return chunk(2 * (chip - i), valid) + chunk(2 * (chip - i) + 1, valid)

    def chip_map(i):
        mine, paired = chip_refs[i][...], chip_refs[i + len(chip_refs) // 2][...]
        first_core = track % 2 == 0
        top, bottom = jnp.where(first_core, mine, paired), jnp.where(first_core, paired, mine)
        return jnp.concatenate([top, bottom], axis=0)

    furthest = n_track // 2 - 1
    entry = chip_end(furthest)
    for i in range(furthest - 1, 0, -1):
        entry = chip_end(i) + times_f32(spread(entry), chip_map(i - 1))
    inside = chunk(track - 1, track > 0) + times_f32(spread(entry), other_ref[...])
    entry = jnp.where(track % 2 == 1, inside, entry)
    entry_ref[...] = entry
    columns = [spread(entry)]
    for q in range(1, CHAINS):
        begin = begins_ref[q - 1 : q, :] + times_f32(columns[0], through_ref[q - 1])
        columns.append(spread(begin))
    even = strip % 2 == 0
    for j in range(cap):
        value = local_ref[j : j + 1, :] + times_f32(columns[j // length], maps_ref[j])
        masked = jnp.where(is_live(pos_ref, j), value, 0.0)
        value_ref[j : j + 1, :] = masked
        crossed = times(split_row(jnp.broadcast_to(masked, (ROWS, width))), coupling_ref[j], NN)[:1]
        first_ref[j : j + 1, :] = jnp.where(even, masked, crossed)
        second_ref[j : j + 1, :] = jnp.where(even, crossed, masked)


def local_kernel(cap, value_ref, entry_ref, diag_ref, lower_ref, links_ref, pos_ref, base_ref):
    lowered = link(links_ref, pos_ref, 0) * times(split_row(wide_row(entry_ref, 0)), lower_ref[0], NT)
    held = None
    for j in range(cap):
        lhs = split_row(wide_row(value_ref, j))
        own = times(lhs, diag_ref[j], NT) + lowered
        if j > 0:
            held = held + link(links_ref, pos_ref, j) * times(lhs, lower_ref[j], NN)
            base_ref[j - 1 : j, :] = held[:1]
        if j < cap - 1:
            lowered = link(links_ref, pos_ref, j + 1) * times(lhs, lower_ref[j + 1], NT)
        held = own
    base_ref[cap - 1 : cap, :] = held[:1]


def alpha_of(recv_ref, half):
    total = jnp.sum(recv_ref[...], axis=0)
    inner = jnp.sum(total[half : half + 1], axis=1, keepdims=True)
    energy = jnp.sum(total[half + 1 : half + 2], axis=1, keepdims=True)
    return inner / (energy + 1e-6)


def update_kernel(
    cap, n_track, n_strip, first, base_ref, first_ref, second_ref, recv_ref, value_ref, state_ref, edge_map_ref, coupling_ref,
    lower_ref, precond_ref, maps_ref, other_ref, links_ref, pos_ref, next_ref, local_ref, begins_ref, send_ref,
):
    track, strip, count = pos_ref[0], pos_ref[1], pos_ref[2]
    width = base_ref.shape[1]
    length = cap // CHAINS
    odd = strip % 2 == 1
    image_ref = next_ref.at[1]
    one, two = first_ref[...], second_ref[...]
    below = jnp.where(strip > 0, jnp.where(odd, one, two), 0.0)
    above = jnp.where(strip < n_strip - 1, jnp.where(odd, two, one), 0.0)
    ahead = recv_ref[strip * n_track + jnp.minimum(track + 1, n_track - 1)]
    ahead = jnp.concatenate([ahead[h : h + 1] for h in range(width // 128)], axis=1)
    ahead = ahead + times_f32(spread(value_ref[pl.ds(count - 1, 1), :]), edge_map_ref[...])
    ahead = jnp.where(track < n_track - 1, ahead, 0.0)
    at_end = lax.broadcasted_iota(jnp.int32, (cap, width), 0) == count - 1
    image_ref[...] = base_ref[...] + above + jnp.where(at_end, ahead, 0.0)
    for j in range(cap):
        row = jnp.broadcast_to(below[j : j + 1, :], (ROWS, width))
        crossed = times(split_row(row), coupling_ref[j], NT)
        image_ref[j : j + 1, :] = image_ref[j : j + 1, :] + crossed[:1]
    mask = live_mask(pos_ref, (cap, width))
    image = jnp.where(mask, image_ref[...], 0.0)
    if first:
        next_ref[0] = jnp.where(mask, state_ref[...], 0.0)
        next_ref[2] = value_ref[...]
        next_ref[3] = jnp.zeros_like(image)
        next_ref[1] = image
    else:
        alpha = alpha_of(recv_ref, width // 128)
        next_ref[0] = state_ref[0] - alpha * state_ref[1]
        next_ref[3] = state_ref[3] + alpha * state_ref[2]
        next_ref[2] = state_ref[2] - alpha * value_ref[...]
        next_ref[1] = state_ref[1] - alpha * image
    dots = dot_parts(next_ref[0], next_ref[1])
    if local_ref is None:
        packed = jnp.concatenate([jnp.zeros((width // 128, 128), F32)] + dots, axis=0)
        for i in range(send_ref.shape[0]):
            send_ref[i] = packed
        return
    state = [None] * CHAINS
    for t in range(length):
        for q in range(CHAINS):
            j = q * length + t
            inner = wide_row(image_ref, j)
            if t > 0:
                lowered = times(split_row(state[q]), lower_ref[j], NT)
                inner = inner - link(links_ref, pos_ref, j) * lowered
            value = times(split_row(inner), precond_ref[j], NT)
            state[q] = jnp.where(is_live(pos_ref, j), value, state[q] if t > 0 else 0.0)
            local_ref[j : j + 1, :] = state[q][:1]
            if j == 0:
                edge = link(links_ref, pos_ref, 0) * times(split_row(state[q]), lower_ref[0], NN)
    ends = chain_ends(state, maps_ref, length)
    begins_ref[...] = jnp.concatenate(ends, axis=0)
    send_ends(ends[-1], edge[:1], dots, other_ref, pos_ref, n_track, send_ref)


def last_update_kernel(cap, n_track, n_strip, *refs):
    update_kernel(cap, n_track, n_strip, False, *refs[:-1], None, None, refs[-1])


def final_kernel(recv_ref, state_ref, solution_ref, residual_ref):
    alpha = alpha_of(recv_ref, state_ref.shape[2] // 128)
    solution_ref[...] = state_ref[3] + alpha * state_ref[2]
    residual_ref[...] = state_ref[0] - alpha * state_ref[1]


def call(kernel, outs, specs, *args, scratch=(), vmem=VMEM_BYTES):
    outs = [out if len(out) == 2 and isinstance(out[0], tuple) else (out, F32) for out in outs]
    args = [
        pltpu.with_memory_space_constraint(arg, spec.memory_space) if arg.size >= PINNED or spec is HBM else arg
        for arg, spec in zip(args, specs)
    ]
    return pl.pallas_call(
        kernel,
        out_shape=[
            pltpu.VMEM(shape, dtype) if math.prod(shape) >= PINNED else jax.ShapeDtypeStruct(shape, dtype)
            for shape, dtype in outs
        ],
        in_specs=specs,
        out_specs=[VMEM] * len(outs),
        scratch_shapes=scratch,
        compiler_params=pltpu.CompilerParams(vmem_limit_bytes=vmem),
    )(*args)


def body(rhs, principal_tiles, lower_blocks, coupling_blocks, precond_blocks, seg_blocks, links):
    cap, width = rhs.shape[1:]
    n_track, n_strip = lax.axis_size("track"), lax.axis_size("strip")
    track, strip = lax.axis_index("track"), lax.axis_index("strip")
    pos = jnp.stack([track, strip, seg_blocks[0]]).astype(jnp.int32)
    rhs = rhs[0]
    whole = n_track * n_strip
    chips = n_track // 2
    block = (cap, width)
    square = (width, width)
    stack = (cap, width, width)
    chunk = (whole, width // 128 + 2, 128)
    chain = (CHAINS, width)
    swap = [(i, i ^ 1) for i in range(n_track)]

    maps, total, edge_map, local, ends, begins, through, lower, precond, diag, coupling = call(
        functools.partial(maps_kernel, cap),
        [stack, square, square, block, (2, width), chain, (CHAINS - 1,) + square] + [(stack, jnp.bfloat16)] * 4,
        [HBM] * 6 + [SMEM],
        rhs, links, lower_blocks[0], precond_blocks[0], principal_tiles[0], coupling_blocks[0], pos,
        scratch=[
            pltpu.VMEM(block, F32), pltpu.SMEM(links.shape, jnp.int32),
            pltpu.SemaphoreType.DMA((4 * CHAINS + 4,)),
        ],
    )
    other = lax.ppermute(total, "track", swap)
    chip, send = call(
        functools.partial(pair_kernel, n_track),
        [(width // 2, width), chunk],
        [VMEM] * 3 + [SMEM] + [VMEM] * 5,
        total, other, ends, pos, maps, lower, precond, diag, coupling,
    )
    nearer = [
        lax.ppermute(chip, "track", [(i, i + 2 * k) for i in range(2, n_track - 2 * k)])
        for k in range(1, chips - 1)
    ]
    state = rhs
    pairs = [(i, i ^ 1) for i in range(n_strip) if i ^ 1 < n_strip]
    cross = [(i, (i + 1 if i % 2 else i - 1) % n_strip) for i in range(n_strip)]
    for step_number in range(ITERS):
        recv = lax.all_to_all(send, ("strip", "track"), 0, 0)
        if step_number == 0:
            recv, *nearer = lax.optimization_barrier((recv, *nearer))
            nearer += [lax.ppermute(part, "track", swap) for part in nearer]
        value, first, second, entry = call(
            functools.partial(direction_kernel, cap, n_track),
            [block, block, block, (1, width)],
            [VMEM] * (7 + len(nearer)) + [SMEM],
            recv, local, begins, maps, through, other, coupling, *nearer, pos,
        )
        if step_number == 0:
            edge_map, entry = lax.optimization_barrier((edge_map, entry))
            edge_map = lax.ppermute(edge_map, "track", [((i + 1) % n_track, i) for i in range(n_track)])
        first = lax.ppermute(first, "strip", pairs)
        second = lax.ppermute(second, "strip", cross)
        base, = call(
            functools.partial(local_kernel, cap),
            [block],
            [VMEM] * 4 + [SMEM] * 2,
            value, entry, diag, lower, links, pos,
        )
        args = (base, first, second, recv, value, state, edge_map, coupling, lower, precond, maps, other, links, pos)
        specs = [VMEM] * 12 + [SMEM] * 2
        if step_number < ITERS - 1:
            kernel = functools.partial(update_kernel, cap, n_track, n_strip, step_number == 0)
            state, local, begins, send = call(kernel, [(4,) + block, block, chain, chunk], specs, *args)
        else:
            kernel = functools.partial(last_update_kernel, cap, n_track, n_strip)
            state, send = call(kernel, [(4,) + block, chunk], specs, *args)
    recv = lax.all_to_all(send, ("strip", "track"), 0, 0)
    solution, residual = call(final_kernel, [block, block], [VMEM] * 2, recv, state)
    return (solution[None], residual[None])


def solution(mesh):
    in_specs = (
        P("strip", "track", None),
        P("strip", "track", None, None),
        P("strip", "track", None, None),
        P("strip", "track", None, None),
        P("strip", "track", None, None),
        P("track"),
        P("strip", "track"),
    )
    out_specs = (P("strip", "track", None), P("strip", "track", None))
    return jax.shard_map(body, mesh=mesh, in_specs=in_specs, out_specs=out_specs, check_vma=False)
```

```python
import functools
import math

import jax
import jax.numpy as jnp
from jax import lax
from jax.experimental import pallas as pl
from jax.experimental.pallas import tpu as pltpu
from jax.sharding import PartitionSpec as P

ITERS = 6
CHAINS = 4
ROWS = 8
EARLY = 1
VMEM_BYTES = 16 * 1024 * 1024
PINNED = 1 << 19
NT = (((1,), (1,)), ((), ()))
NN = (((1,), (0,)), ((), ()))
VMEM = pl.BlockSpec(memory_space=pltpu.VMEM)
HBM = pl.BlockSpec(memory_space=pltpu.MemorySpace.HBM)
SMEM = pl.BlockSpec(memory_space=pltpu.SMEM)
F32 = jnp.float32


def pieces(value):
    high = value.astype(jnp.bfloat16)
    rest = value - high.astype(F32)
    middle = rest.astype(jnp.bfloat16)
    low = (rest - middle.astype(F32)).astype(jnp.bfloat16)
    return jnp.concatenate([high, middle, low], axis=0)


def split_row(row):
    return pieces(jnp.concatenate([row, row], axis=0))


def times(lhs, matrix, dims):
    out = lax.dot_general(lhs, matrix, dims, preferred_element_type=F32)
    return out[:ROWS] + out[2 * ROWS : 3 * ROWS] + out[4 * ROWS : 5 * ROWS]


def times_matrix(value, matrix, dims):
    out = lax.dot_general(pieces(value), matrix, dims, preferred_element_type=F32)
    n = value.shape[0]
    return out[:n] + out[n : 2 * n] + out[2 * n :]


def spread(row):
    return jnp.transpose(jnp.broadcast_to(row, (128, row.shape[1])))


def times_f32(column, matrix):
    wide = jnp.concatenate([column] * (matrix.shape[1] // 128), axis=1)
    return jnp.sum(matrix * wide, axis=0, keepdims=True)


def wide_row(ref, j):
    return jnp.broadcast_to(ref[j : j + 1, :], (ROWS, ref.shape[1]))


def is_live(pos_ref, j):
    return j < pos_ref[2]


def link(links_ref, pos_ref, j):
    joined = links_ref[0, j] if j else jnp.where(pos_ref[0] > 0, links_ref[0, 0], 0)
    return jnp.where(is_live(pos_ref, j), joined, 0).astype(F32)


def live_mask(pos_ref, shape):
    return lax.broadcasted_iota(jnp.int32, shape, 0) < pos_ref[2]


def dot_parts(residual, image):
    parts = []
    for left in (residual, image):
        partial = jnp.sum(left * image, axis=0, keepdims=True)
        parts.append(sum(partial[:, i : i + 128] for i in range(0, partial.shape[1], 128)))
    return parts


def halves(row):
    return [row[:, i : i + 128] for i in range(0, row.shape[1], 128)]


def send_ends(end, first, dots, other_ref, pos_ref, n_track, out_ref):
    track = pos_ref[0]
    carried = jnp.where(track % 2 == 0, times_f32(spread(end), other_ref[...]), end)
    near = jnp.concatenate(halves(end) + dots, axis=0)
    far = jnp.concatenate(halves(carried) + dots, axis=0)
    back = jnp.concatenate(halves(first) + dots, axis=0)
    for i in range(out_ref.shape[0]):
        ahead = i % n_track - track
        out_ref[i] = jnp.where(ahead > 1, far, jnp.where(ahead == 1, near, back))


def chain_ends(state, maps_ref, length):
    ends = [state[0][:1]]
    for q in range(1, CHAINS):
        ends.append(state[q][:1] + times_f32(spread(ends[-1]), maps_ref[q * length + length - 1]))
    return ends


def maps_kernel(
    cap, rhs_hbm, links_hbm, lower_hbm, precond_hbm, diag_hbm, coupling_hbm, pos_ref,
    maps_ref, total_ref, edge_ref, local_ref, ends_ref, begins_ref, through_ref,
    lower_ref, precond_ref, diag_ref, coupling_ref,
    rhs_ref, links_ref, sems,
):
    width = lower_ref.shape[-1]
    length = cap // CHAINS
    copies = [
        pltpu.make_async_copy(rhs_hbm, rhs_ref, sems.at[0]),
        pltpu.make_async_copy(links_hbm, links_ref, sems.at[1]),
    ]

    def load(source, target, start, count):
        rows = pl.ds(start, count)
        copies.append(pltpu.make_async_copy(source.at[rows], target.at[rows], sems.at[len(copies)]))

    for begin, end in ((0, EARLY), (EARLY, length)):
        for source, target in ((lower_hbm, lower_ref), (precond_hbm, precond_ref)):
            for q in range(CHAINS):
                load(source, target, q * length + begin, end - begin)
    load(diag_hbm, diag_ref, 0, cap)
    load(coupling_hbm, coupling_ref, 0, cap)
    for copy in copies:
        copy.start()
    early = 2 + 2 * CHAINS
    for copy in copies[:early]:
        copy.wait()
    rows = lax.broadcasted_iota(jnp.int32, (width, width), 0)
    cols = lax.broadcasted_iota(jnp.int32, (width, width), 1)
    ident = jnp.where(rows == cols, 1.0, 0.0).astype(F32)
    state = [ident] * CHAINS
    local = [None] * CHAINS
    for t in range(length):
        if t == EARLY:
            for copy in copies[early:-2]:
                copy.wait()
        for q in range(CHAINS):
            j = q * length + t
            live, on = is_live(pos_ref, j), link(links_ref, pos_ref, j)
            if t == 0:
                inner = lax.dot_general(
                    ident.astype(jnp.bfloat16), lower_ref[j], NT, preferred_element_type=F32
                )
                value = lax.dot_general(
                    inner.astype(jnp.bfloat16), precond_ref[j], NT, preferred_element_type=F32
                )
            else:
                inner = times_matrix(state[q], lower_ref[j], NT)
                value = times_matrix(inner, precond_ref[j], NT)
            state[q] = jnp.where(live, -on * value, state[q])
            maps_ref[j] = state[q]
            inner = wide_row(rhs_ref, j)
            if t > 0:
                inner = inner - on * times(split_row(local[q]), lower_ref[j], NT)
            value = times(split_row(inner), precond_ref[j], NT)
            local[q] = jnp.where(live, value, local[q] if t > 0 else 0.0)
            local_ref[j : j + 1, :] = local[q][:1]
            if j == 0:
                edge_ref[...] = times_matrix(state[q], lower_ref[0], NN)
                ends_ref[1:2, :] = (on * times(split_row(local[q]), lower_ref[0], NN))[:1]
    span = 1
    while span < CHAINS:
        state = [
            state[q] if q < span else jnp.dot(state[q - span], state[q], precision=lax.Precision.HIGHEST)
            for q in range(CHAINS)
        ]
        span *= 2
    for q in range(CHAINS - 1):
        through_ref[q] = state[q]
    total_ref[...] = state[-1]
    ends = chain_ends(local, maps_ref, length)
    ends_ref[0:1, :] = ends[-1]
    begins_ref[...] = jnp.concatenate(ends, axis=0)
    for copy in copies[-2:]:
        copy.wait()


def pair_kernel(n_track, total_ref, other_ref, ends_ref, pos_ref, *refs):
    chip_ref, send_ref = refs[-2:]
    first_core = pos_ref[0] % 2 == 0
    own, other = total_ref[...], other_ref[...]
    half = own.shape[0] // 2
    early = jnp.where(first_core, own[:half], other[half:])
    late = jnp.where(first_core, other, own)
    chip_ref[...] = jnp.dot(early, late, precision=lax.Precision.HIGHEST)
    dots = [jnp.zeros((1, 128), F32)] * 2
    send_ends(ends_ref[0:1, :], ends_ref[1:2, :], dots, other_ref, pos_ref, n_track, send_ref)


def direction_kernel(cap, n_track, recv_ref, local_ref, begins_ref, maps_ref, through_ref, other_ref, coupling_ref, *refs):
    chip_refs, (pos_ref, value_ref, first_ref, second_ref, entry_ref) = refs[:-5], refs[-5:]
    track, strip = pos_ref[0], pos_ref[1]
    width = local_ref.shape[1]
    length = cap // CHAINS
    half = width // 128
    base = strip * n_track
    chip = track // 2

    def chunk(index, valid):
        got = recv_ref[base + jnp.clip(index, 0, n_track - 1)]
        got = jnp.where(valid, got, 0.0)
        return jnp.concatenate([got[h : h + 1] for h in range(half)], axis=1)

    def chip_end(i):
        valid = chip - i >= 0
        return chunk(2 * (chip - i), valid) + chunk(2 * (chip - i) + 1, valid)

    def chip_map(i):
        mine, paired = chip_refs[i][...], chip_refs[i + len(chip_refs) // 2][...]
        first_core = track % 2 == 0
        top, bottom = jnp.where(first_core, mine, paired), jnp.where(first_core, paired, mine)
        return jnp.concatenate([top, bottom], axis=0)

    furthest = n_track // 2 - 1
    entry = chip_end(furthest)
    for i in range(furthest - 1, 0, -1):
        entry = chip_end(i) + times_f32(spread(entry), chip_map(i - 1))
    inside = chunk(track - 1, track > 0) + times_f32(spread(entry), other_ref[...])
    entry = jnp.where(track % 2 == 1, inside, entry)
    entry_ref[...] = entry
    columns = [spread(entry)]
    for q in range(1, CHAINS):
        begin = begins_ref[q - 1 : q, :] + times_f32(columns[0], through_ref[q - 1])
        columns.append(spread(begin))
    even = strip % 2 == 0
    for j in range(cap):
        value = local_ref[j : j + 1, :] + times_f32(columns[j // length], maps_ref[j])
        masked = jnp.where(is_live(pos_ref, j), value, 0.0)
        value_ref[j : j + 1, :] = masked
        crossed = times(split_row(jnp.broadcast_to(masked, (ROWS, width))), coupling_ref[j], NN)[:1]
        first_ref[j : j + 1, :] = jnp.where(even, masked, crossed)
        second_ref[j : j + 1, :] = jnp.where(even, crossed, masked)


def flip_kernel(cap, *refs):
    sources, targets = refs[: len(refs) // 2], refs[len(refs) // 2 :]
    for source, target in zip(sources, targets):
        for j in range(cap):
            target[j] = jnp.transpose(source[j])


def alpha_of(recv_ref, half):
    total = jnp.sum(recv_ref[...], axis=0)
    inner = jnp.sum(total[half : half + 1], axis=1, keepdims=True)
    energy = jnp.sum(total[half + 1 : half + 2], axis=1, keepdims=True)
    return inner / (energy + 1e-6)


def local_kernel(
    cap, first, value_ref, entry_ref, recv_ref, state_ref, image_ref, diag_flip_ref, lower_ref,
    lower_flip_ref, links_ref, pos_ref, base_ref, next_ref, alpha_ref,
):
    width = value_ref.shape[1]
    on = [link(links_ref, pos_ref, j) for j in range(cap)]
    lowered = on[0] * times(split_row(wide_row(entry_ref, 0)), lower_flip_ref[0], NN)
    held = None
    for j in range(cap):
        lhs = split_row(wide_row(value_ref, j))
        own = times(lhs, diag_flip_ref[j], NN) + lowered
        if j > 0:
            held = held + on[j] * times(lhs, lower_ref[j], NN)
            base_ref[j - 1 : j, :] = held[:1]
        if j < cap - 1:
            lowered = on[j + 1] * times(lhs, lower_flip_ref[j + 1], NN)
        held = own
    base_ref[cap - 1 : cap, :] = held[:1]
    if first:
        next_ref[0] = jnp.where(live_mask(pos_ref, (cap, width)), state_ref[...], 0.0)
        next_ref[1] = value_ref[...]
        next_ref[2] = jnp.zeros_like(value_ref[...])
        alpha_ref[...] = jnp.zeros((1, width), F32)
    else:
        alpha = alpha_of(recv_ref, width // 128)
        next_ref[0] = state_ref[0] - alpha * image_ref[...]
        next_ref[1] = state_ref[1] - alpha * value_ref[...]
        next_ref[2] = state_ref[2] + alpha * state_ref[1]
        alpha_ref[...] = jnp.broadcast_to(alpha, (1, width))


def update_kernel(
    cap, n_track, n_strip, first, base_ref, first_ref, second_ref, value_ref, recv_ref, state_ref, image_ref, alpha_ref,
    edge_map_ref, coupling_flip_ref, lower_ref, lower_flip_ref, precond_flip_ref, maps_ref, other_ref, links_ref, pos_ref,
    next_ref, local_ref, begins_ref, send_ref,
):
    track, strip, count = pos_ref[0], pos_ref[1], pos_ref[2]
    width = base_ref.shape[1]
    length = cap // CHAINS
    odd = strip % 2 == 1
    one, two = first_ref[...], second_ref[...]
    below = jnp.where(strip > 0, jnp.where(odd, one, two), 0.0)
    above = jnp.where(strip < n_strip - 1, jnp.where(odd, two, one), 0.0)
    ahead = recv_ref[strip * n_track + jnp.minimum(track + 1, n_track - 1)]
    ahead = jnp.concatenate([ahead[h : h + 1] for h in range(width // 128)], axis=1)
    ahead = ahead + times_f32(spread(value_ref[pl.ds(count - 1, 1), :]), edge_map_ref[...])
    ahead = jnp.where(track < n_track - 1, ahead, 0.0)
    at_end = lax.broadcasted_iota(jnp.int32, (cap, width), 0) == count - 1
    known = base_ref[...] + above + jnp.where(at_end, ahead, 0.0)
    alpha = alpha_ref[...]
    for j in range(cap):
        crossed = times(split_row(wide_row(below, j)), coupling_flip_ref[j], NN)
        next_ref[j : j + 1, :] = known[j : j + 1, :] + crossed[:1]
    image = jnp.where(live_mask(pos_ref, (cap, width)), next_ref[...], 0.0)
    next_ref[...] = image if first else image_ref[...] - alpha * image
    state = [None] * CHAINS
    steps = range(0 if local_ref is None else length)
    for t in steps:
        inner = []
        for q in range(CHAINS):
            j = q * length + t
            inner.append(wide_row(next_ref, j))
            if t > 0:
                lowered = times(split_row(state[q]), lower_flip_ref[j], NN)
                inner[q] = inner[q] - link(links_ref, pos_ref, j) * lowered
        for q in range(CHAINS):
            j = q * length + t
            value = times(split_row(inner[q]), precond_flip_ref[j], NN)
            state[q] = jnp.where(is_live(pos_ref, j), value, state[q] if t > 0 else 0.0)
            local_ref[j : j + 1, :] = state[q][:1]
            if j == 0:
                edge = link(links_ref, pos_ref, 0) * times(split_row(state[q]), lower_ref[0], NN)
    dots = dot_parts(state_ref[0], next_ref[...])
    if local_ref is None:
        packed = jnp.concatenate([jnp.zeros((width // 128, 128), F32)] + dots, axis=0)
        for i in range(send_ref.shape[0]):
            send_ref[i] = packed
        return
    ends = chain_ends(state, maps_ref, length)
    begins_ref[...] = jnp.concatenate(ends, axis=0)
    send_ends(ends[-1], edge[:1], dots, other_ref, pos_ref, n_track, send_ref)


def last_update_kernel(cap, n_track, n_strip, *refs):
    update_kernel(cap, n_track, n_strip, False, *refs[:-1], None, None, refs[-1])


def final_kernel(recv_ref, state_ref, image_ref, solution_ref, residual_ref):
    alpha = alpha_of(recv_ref, state_ref.shape[2] // 128)
    solution_ref[...] = state_ref[2] + alpha * state_ref[1]
    residual_ref[...] = state_ref[0] - alpha * image_ref[...]


def call(kernel, outs, specs, *args, scratch=(), vmem=VMEM_BYTES):
    outs = [out if len(out) == 2 and isinstance(out[0], tuple) else (out, F32) for out in outs]
    args = [
        pltpu.with_memory_space_constraint(arg, spec.memory_space) if arg.size >= PINNED or spec is HBM else arg
        for arg, spec in zip(args, specs)
    ]
    return pl.pallas_call(
        kernel,
        out_shape=[
            pltpu.VMEM(shape, dtype) if math.prod(shape) >= PINNED else jax.ShapeDtypeStruct(shape, dtype)
            for shape, dtype in outs
        ],
        in_specs=specs,
        out_specs=[VMEM] * len(outs),
        scratch_shapes=scratch,
        compiler_params=pltpu.CompilerParams(vmem_limit_bytes=vmem),
    )(*args)


def body(rhs, principal_tiles, lower_blocks, coupling_blocks, precond_blocks, seg_blocks, links):
    cap, width = rhs.shape[1:]
    n_track, n_strip = lax.axis_size("track"), lax.axis_size("strip")
    track, strip = lax.axis_index("track"), lax.axis_index("strip")
    pos = jnp.stack([track, strip, seg_blocks[0]]).astype(jnp.int32)
    rhs = rhs[0]
    whole = n_track * n_strip
    chips = n_track // 2
    block = (cap, width)
    square = (width, width)
    stack = (cap, width, width)
    chunk = (whole, width // 128 + 2, 128)
    chain = (CHAINS, width)
    swap = [(i, i ^ 1) for i in range(n_track)]

    def flip(*stacks):
        kernel = functools.partial(flip_kernel, cap)
        return call(kernel, [(stack, jnp.bfloat16)] * len(stacks), [VMEM] * len(stacks), *stacks)

    maps, total, edge_map, local, ends, begins, through, lower, precond, diag, coupling = call(
        functools.partial(maps_kernel, cap),
        [stack, square, square, block, (2, width), chain, (CHAINS - 1,) + square] + [(stack, jnp.bfloat16)] * 4,
        [HBM] * 6 + [SMEM],
        rhs, links, lower_blocks[0], precond_blocks[0], principal_tiles[0], coupling_blocks[0], pos,
        scratch=[
            pltpu.VMEM(block, F32), pltpu.SMEM(links.shape, jnp.int32),
            pltpu.SemaphoreType.DMA((4 * CHAINS + 4,)),
        ],
    )
    other = lax.ppermute(total, "track", swap)
    lower_flip, precond_flip = flip(lower, precond)
    chip, send = call(
        functools.partial(pair_kernel, n_track),
        [(width // 2, width), chunk],
        [VMEM] * 3 + [SMEM] + [VMEM] * 6,
        total, other, ends, pos, maps, lower, lower_flip, precond_flip, diag, coupling,
    )
    nearer = [
        lax.ppermute(
            chip, "track", swap[:2] + [(i, 2 + (i - 2 + 2 * k) % (n_track - 2)) for i in range(2, n_track)]
        )
        for k in range(1, chips - 1)
    ]
    state = image = rhs
    pairs = [(i, i ^ 1) for i in range(n_strip) if i ^ 1 < n_strip]
    cross = []
    for d in range(n_track):
        for i in range(n_strip):
            partner = i + 1 if i % 2 else i - 1
            if 0 <= partner < n_strip:
                cross.append((d * n_strip + i, d * n_strip + partner))
            else:
                cross.append((d * n_strip + i, (d ^ 1) * n_strip + i))
    for step_number in range(ITERS):
        recv = lax.all_to_all(send, ("strip", "track"), 0, 0)
        if step_number == 0:
            recv, diag, coupling, *nearer = lax.optimization_barrier((recv, diag, coupling, *nearer))
            nearer += [lax.ppermute(part, "track", swap) for part in nearer]
            diag_flip, coupling_flip = flip(diag, coupling)
        value, first, second, entry = call(
            functools.partial(direction_kernel, cap, n_track),
            [block, block, block, (1, width)],
            [VMEM] * (7 + len(nearer)) + [SMEM],
            recv, local, begins, maps, through, other, coupling, *nearer, pos,
        )
        if step_number == 0:
            edge_map, entry = lax.optimization_barrier((edge_map, entry))
            edge_map = lax.ppermute(edge_map, "track", [((i + 1) % n_track, i) for i in range(n_track)])
        first = lax.ppermute(first, "strip", pairs)
        second = lax.ppermute(second, ("track", "strip"), cross)
        base, state, alpha = call(
            functools.partial(local_kernel, cap, step_number == 0),
            [block, (3,) + block, (1, width)],
            [VMEM] * 8 + [SMEM] * 2,
            value, entry, recv, state, image, diag_flip, lower, lower_flip, links, pos,
        )
        args = (
            base, first, second, value, recv, state, image, alpha, edge_map, coupling_flip, lower, lower_flip,
            precond_flip, maps, other, links, pos,
        )
        specs = [VMEM] * 15 + [SMEM] * 2
        if step_number < ITERS - 1:
            kernel = functools.partial(update_kernel, cap, n_track, n_strip, step_number == 0)
            image, local, begins, send = call(kernel, [block, block, chain, chunk], specs, *args)
        else:
            kernel = functools.partial(last_update_kernel, cap, n_track, n_strip)
            image, send = call(kernel, [block, chunk], specs, *args)
    recv = lax.all_to_all(send, ("strip", "track"), 0, 0)
    solution, residual = call(final_kernel, [block, block], [VMEM] * 3, recv, state, image)
    return (solution[None], residual[None])


def solution(mesh):
    in_specs = (
        P("strip", "track", None),
        P("strip", "track", None, None),
        P("strip", "track", None, None),
        P("strip", "track", None, None),
        P("strip", "track", None, None),
        P("track"),
        P("strip", "track"),
    )
    out_specs = (P("strip", "track", None), P("strip", "track", None))
    return jax.shard_map(body, mesh=mesh, in_specs=in_specs, out_specs=out_specs, check_vma=False)
```

```python
import functools
import math

import jax
import jax.numpy as jnp
from jax import lax
from jax.experimental import pallas as pl
from jax.experimental.pallas import tpu as pltpu
from jax.sharding import PartitionSpec as P

ITERS = 6
CHAINS = 4
ROWS = 8
EARLY = 1
VMEM_BYTES = 16 * 1024 * 1024
PINNED = 1 << 19
NT = (((1,), (1,)), ((), ()))
NN = (((1,), (0,)), ((), ()))
VMEM = pl.BlockSpec(memory_space=pltpu.VMEM)
HBM = pl.BlockSpec(memory_space=pltpu.MemorySpace.HBM)
SMEM = pl.BlockSpec(memory_space=pltpu.SMEM)
F32 = jnp.float32


def pieces(value):
    high = value.astype(jnp.bfloat16)
    rest = value - high.astype(F32)
    middle = rest.astype(jnp.bfloat16)
    low = (rest - middle.astype(F32)).astype(jnp.bfloat16)
    return jnp.concatenate([high, middle, low], axis=0)


def split_row(row):
    return pieces(jnp.concatenate([row, row], axis=0))


def times(lhs, matrix, dims):
    out = lax.dot_general(lhs, matrix, dims, preferred_element_type=F32)
    return out[:ROWS] + out[2 * ROWS : 3 * ROWS] + out[4 * ROWS : 5 * ROWS]


def times_matrix(value, matrix, dims):
    out = lax.dot_general(pieces(value), matrix, dims, preferred_element_type=F32)
    n = value.shape[0]
    return out[:n] + out[n : 2 * n] + out[2 * n :]


def spread(row):
    return jnp.transpose(jnp.broadcast_to(row, (128, row.shape[1])))


def times_f32(column, matrix):
    wide = jnp.concatenate([column] * (matrix.shape[1] // 128), axis=1)
    return jnp.sum(matrix * wide, axis=0, keepdims=True)


def wide_row(ref, j):
    return jnp.broadcast_to(ref[j : j + 1, :], (ROWS, ref.shape[1]))


def is_live(pos_ref, j):
    return j < pos_ref[2]


def link(links_ref, pos_ref, j):
    joined = links_ref[0, j] if j else jnp.where(pos_ref[0] > 0, links_ref[0, 0], 0)
    return jnp.where(is_live(pos_ref, j), joined, 0).astype(F32)


def live_mask(pos_ref, shape):
    return lax.broadcasted_iota(jnp.int32, shape, 0) < pos_ref[2]


def dot_parts(residual, image):
    parts = []
    for left in (residual, image):
        partial = jnp.sum(left * image, axis=0, keepdims=True)
        parts.append(sum(partial[:, i : i + 128] for i in range(0, partial.shape[1], 128)))
    return parts


def halves(row):
    return [row[:, i : i + 128] for i in range(0, row.shape[1], 128)]


def send_ends(end, first, dots, other_ref, pos_ref, n_track, out_ref):
    track = pos_ref[0]
    carried = jnp.where(track % 2 == 0, times_f32(spread(end), other_ref[...]), end)
    near = jnp.concatenate(halves(end) + dots, axis=0)
    far = jnp.concatenate(halves(carried) + dots, axis=0)
    back = jnp.concatenate(halves(first) + dots, axis=0)
    for i in range(out_ref.shape[0]):
        ahead = i % n_track - track
        out_ref[i] = jnp.where(ahead > 1, far, jnp.where(ahead == 1, near, back))


def chain_ends(state, maps_ref, last_two_ref, length):
    ends = [state[0][:1]]
    for q in range(1, CHAINS - 1):
        ends.append(state[q][:1] + times_f32(spread(ends[-1]), maps_ref[q * length + length - 1]))
    last = state[-1][:1] + times_f32(spread(state[-2][:1]), maps_ref[CHAINS * length - 1])
    ends.append(last + times_f32(spread(ends[-2]), last_two_ref[...]))
    return ends


def maps_kernel(
    cap, rhs_hbm, links_hbm, lower_hbm, precond_hbm, diag_hbm, coupling_hbm, pos_ref,
    maps_ref, total_ref, edge_ref, local_ref, ends_ref, begins_ref, through_ref, last_two_ref,
    lower_ref, precond_ref, diag_ref, coupling_ref,
    rhs_ref, links_ref, sems,
):
    width = lower_ref.shape[-1]
    length = cap // CHAINS
    copies = [
        pltpu.make_async_copy(rhs_hbm, rhs_ref, sems.at[0]),
        pltpu.make_async_copy(links_hbm, links_ref, sems.at[1]),
    ]

    def load(source, target, start, count):
        rows = pl.ds(start, count)
        copies.append(pltpu.make_async_copy(source.at[rows], target.at[rows], sems.at[len(copies)]))

    for begin, end in ((0, EARLY), (EARLY, length)):
        for source, target in ((lower_hbm, lower_ref), (precond_hbm, precond_ref)):
            for q in range(CHAINS):
                load(source, target, q * length + begin, end - begin)
    load(diag_hbm, diag_ref, 0, cap)
    load(coupling_hbm, coupling_ref, 0, cap)
    for copy in copies:
        copy.start()
    early = 2 + 2 * CHAINS
    for copy in copies[:early]:
        copy.wait()
    rows = lax.broadcasted_iota(jnp.int32, (width, width), 0)
    cols = lax.broadcasted_iota(jnp.int32, (width, width), 1)
    ident = jnp.where(rows == cols, 1.0, 0.0).astype(F32)
    state = [ident] * CHAINS
    local = [None] * CHAINS
    for t in range(length):
        if t == EARLY:
            for copy in copies[early:-2]:
                copy.wait()
        for q in range(CHAINS):
            j = q * length + t
            live, on = is_live(pos_ref, j), link(links_ref, pos_ref, j)
            if t == 0:
                inner = lax.dot_general(
                    ident.astype(jnp.bfloat16), lower_ref[j], NT, preferred_element_type=F32
                )
                value = lax.dot_general(
                    inner.astype(jnp.bfloat16), precond_ref[j], NT, preferred_element_type=F32
                )
            else:
                inner = times_matrix(state[q], lower_ref[j], NT)
                value = times_matrix(inner, precond_ref[j], NT)
            state[q] = jnp.where(live, -on * value, state[q])
            maps_ref[j] = state[q]
            inner = wide_row(rhs_ref, j)
            if t > 0:
                inner = inner - on * times(split_row(local[q]), lower_ref[j], NT)
            value = times(split_row(inner), precond_ref[j], NT)
            local[q] = jnp.where(live, value, local[q] if t > 0 else 0.0)
            local_ref[j : j + 1, :] = local[q][:1]
            if j == 0:
                edge_ref[...] = times_matrix(state[q], lower_ref[0], NN)
                ends_ref[1:2, :] = (on * times(split_row(local[q]), lower_ref[0], NN))[:1]
    span = 1
    while span < CHAINS:
        state = [
            state[q] if q < span else jnp.dot(state[q - span], state[q], precision=lax.Precision.HIGHEST)
            for q in range(CHAINS)
        ]
        if span == 1:
            last_two_ref[...] = state[-1]
        span *= 2
    for q in range(CHAINS - 1):
        through_ref[q] = state[q]
    total_ref[...] = state[-1]
    ends = chain_ends(local, maps_ref, last_two_ref, length)
    ends_ref[0:1, :] = ends[-1]
    begins_ref[...] = jnp.concatenate(ends, axis=0)
    for copy in copies[-2:]:
        copy.wait()


def pair_kernel(n_track, total_ref, other_ref, ends_ref, pos_ref, *refs):
    chip_ref, send_ref = refs[-2:]
    first_core = pos_ref[0] % 2 == 0
    own, other = total_ref[...], other_ref[...]
    early, late = jnp.where(first_core, own, other), jnp.where(first_core, other, own)
    chip_ref[...] = jnp.dot(early, late, precision=lax.Precision.HIGHEST)
    dots = [jnp.zeros((1, 128), F32)] * 2
    send_ends(ends_ref[0:1, :], ends_ref[1:2, :], dots, other_ref, pos_ref, n_track, send_ref)


def direction_kernel(cap, n_track, recv_ref, local_ref, begins_ref, maps_ref, through_ref, other_ref, coupling_ref, *refs):
    chip_refs, (pos_ref, value_ref, first_ref, second_ref, entry_ref) = refs[:-5], refs[-5:]
    track, strip = pos_ref[0], pos_ref[1]
    width = local_ref.shape[1]
    length = cap // CHAINS
    half = width // 128
    base = strip * n_track
    chip = track // 2

    def chunk(index, valid):
        got = recv_ref[base + jnp.clip(index, 0, n_track - 1)]
        got = jnp.where(valid, got, 0.0)
        return jnp.concatenate([got[h : h + 1] for h in range(half)], axis=1)

    def chip_end(i):
        valid = chip - i >= 0
        return chunk(2 * (chip - i), valid) + chunk(2 * (chip - i) + 1, valid)

    def chip_map(i):
        mine, paired = chip_refs[i // 2][...], chip_refs[i // 2 + len(chip_refs) // 2][...]
        return jnp.where(track % 2 == i % 2, mine, paired)

    furthest = n_track // 2 - 1
    entry = chip_end(furthest)
    for i in range(furthest - 1, 0, -1):
        entry = chip_end(i) + times_f32(spread(entry), chip_map(i - 1))
    inside = chunk(track - 1, track > 0) + times_f32(spread(entry), other_ref[...])
    entry = jnp.where(track % 2 == 1, inside, entry)
    entry_ref[...] = entry
    columns = [spread(entry)]
    for q in range(1, CHAINS):
        begin = begins_ref[q - 1 : q, :] + times_f32(columns[0], through_ref[q - 1])
        columns.append(spread(begin))
    even = strip % 2 == 0
    for j in range(cap):
        value = local_ref[j : j + 1, :] + times_f32(columns[j // length], maps_ref[j])
        masked = jnp.where(is_live(pos_ref, j), value, 0.0)
        value_ref[j : j + 1, :] = masked
        crossed = times(split_row(jnp.broadcast_to(masked, (ROWS, width))), coupling_ref[j], NN)[:1]
        first_ref[j : j + 1, :] = jnp.where(even, masked, crossed)
        second_ref[j : j + 1, :] = jnp.where(even, crossed, masked)


def flip_kernel(cap, *refs):
    sources, targets = refs[: len(refs) // 2], refs[len(refs) // 2 :]
    for source, target in zip(sources, targets):
        for j in range(cap):
            target[j] = jnp.transpose(source[j])


def alpha_of(recv_ref):
    total = jnp.sum(recv_ref[...], axis=0)
    inner = jnp.sum(total[-2:-1], axis=1, keepdims=True)
    energy = jnp.sum(total[-1:], axis=1, keepdims=True)
    return inner / (energy + 1e-6)


def local_kernel(
    cap, first, value_ref, entry_ref, recv_ref, state_ref, image_ref, diag_flip_ref, lower_ref,
    lower_flip_ref, links_ref, pos_ref, base_ref, next_ref, alpha_ref,
):
    width = value_ref.shape[1]
    on = [link(links_ref, pos_ref, j) for j in range(cap)]
    lowered = on[0] * times(split_row(wide_row(entry_ref, 0)), lower_flip_ref[0], NN)
    held = None
    for j in range(cap):
        lhs = split_row(wide_row(value_ref, j))
        own = times(lhs, diag_flip_ref[j], NN) + lowered
        if j > 0:
            held = held + on[j] * times(lhs, lower_ref[j], NN)
            base_ref[j - 1 : j, :] = held[:1]
        if j < cap - 1:
            lowered = on[j + 1] * times(lhs, lower_flip_ref[j + 1], NN)
        held = own
    base_ref[cap - 1 : cap, :] = held[:1]
    if first:
        next_ref[0] = jnp.where(live_mask(pos_ref, (cap, width)), state_ref[...], 0.0)
        next_ref[1] = value_ref[...]
        next_ref[2] = jnp.zeros_like(value_ref[...])
        alpha_ref[...] = jnp.zeros((1, width), F32)
    else:
        alpha = alpha_of(recv_ref)
        next_ref[0] = state_ref[0] - alpha * image_ref[...]
        next_ref[1] = state_ref[1] - alpha * value_ref[...]
        next_ref[2] = state_ref[2] + alpha * state_ref[1]
        alpha_ref[...] = jnp.broadcast_to(alpha, (1, width))


def update_kernel(
    cap, n_track, n_strip, first, base_ref, first_ref, second_ref, value_ref, recv_ref, state_ref, image_ref, alpha_ref,
    edge_map_ref, coupling_flip_ref, lower_ref, lower_flip_ref, precond_flip_ref, maps_ref, last_two_ref, other_ref, links_ref, pos_ref,
    next_ref, local_ref, begins_ref, send_ref,
):
    track, strip, count = pos_ref[0], pos_ref[1], pos_ref[2]
    width = base_ref.shape[1]
    length = cap // CHAINS
    odd = strip % 2 == 1
    one, two = first_ref[...], second_ref[...]
    below = jnp.where(strip > 0, jnp.where(odd, one, two), 0.0)
    above = jnp.where(strip < n_strip - 1, jnp.where(odd, two, one), 0.0)
    ahead = recv_ref[strip * n_track + jnp.minimum(track + 1, n_track - 1)]
    ahead = jnp.concatenate([ahead[h : h + 1] for h in range(width // 128)], axis=1)
    ahead = ahead + times_f32(spread(value_ref[pl.ds(count - 1, 1), :]), edge_map_ref[...])
    ahead = jnp.where(track < n_track - 1, ahead, 0.0)
    at_end = lax.broadcasted_iota(jnp.int32, (cap, width), 0) == count - 1
    known = base_ref[...] + above + jnp.where(at_end, ahead, 0.0)
    alpha = wide_row(alpha_ref, 0)

    def image_row(j):
        row = wide_row(known, j) + times(split_row(wide_row(below, j)), coupling_flip_ref[j], NN)
        row = jnp.where(is_live(pos_ref, j), row, 0.0)
        row = row if first else wide_row(image_ref, j) - alpha * row
        next_ref[j : j + 1, :] = row[:1]
        return row

    state = [None] * CHAINS
    rows = [image_row(q * length) for q in range(CHAINS)]
    for t in range(length):
        if local_ref is not None and t > 0:
            for q in range(CHAINS):
                j = q * length + t
                lowered = times(split_row(state[q]), lower_flip_ref[j], NN)
                rows[q] = rows[q] - link(links_ref, pos_ref, j) * lowered
        later = [image_row(q * length + t + 1) for q in range(CHAINS)] if t + 1 < length else []
        for q in range(0 if local_ref is None else CHAINS):
            j = q * length + t
            value = times(split_row(rows[q]), precond_flip_ref[j], NN)
            state[q] = jnp.where(is_live(pos_ref, j), value, state[q] if t > 0 else 0.0)
            local_ref[j : j + 1, :] = state[q][:1]
            if j == 0:
                edge = link(links_ref, pos_ref, 0) * times(split_row(state[q]), lower_ref[0], NN)
        rows = later
    dots = dot_parts(state_ref[0], next_ref[...])
    if local_ref is None:
        packed = jnp.concatenate(dots, axis=0)
        for i in range(send_ref.shape[0]):
            send_ref[i] = packed
        return
    ends = chain_ends(state, maps_ref, last_two_ref, length)
    begins_ref[...] = jnp.concatenate(ends, axis=0)
    send_ends(ends[-1], edge[:1], dots, other_ref, pos_ref, n_track, send_ref)


def last_update_kernel(cap, n_track, n_strip, *refs):
    update_kernel(cap, n_track, n_strip, False, *refs[:-1], None, None, refs[-1])


def final_kernel(recv_ref, state_ref, image_ref, solution_ref, residual_ref):
    alpha = alpha_of(recv_ref)
    solution_ref[...] = state_ref[2] + alpha * state_ref[1]
    residual_ref[...] = state_ref[0] - alpha * image_ref[...]


def call(kernel, outs, specs, *args, scratch=(), vmem=VMEM_BYTES):
    outs = [out if len(out) == 2 and isinstance(out[0], tuple) else (out, F32) for out in outs]
    args = [
        pltpu.with_memory_space_constraint(arg, spec.memory_space) if arg.size >= PINNED or spec is HBM else arg
        for arg, spec in zip(args, specs)
    ]
    return pl.pallas_call(
        kernel,
        out_shape=[
            pltpu.VMEM(shape, dtype) if math.prod(shape) >= PINNED else jax.ShapeDtypeStruct(shape, dtype)
            for shape, dtype in outs
        ],
        in_specs=specs,
        out_specs=[VMEM] * len(outs),
        scratch_shapes=scratch,
        compiler_params=pltpu.CompilerParams(vmem_limit_bytes=vmem),
    )(*args)


def body(rhs, principal_tiles, lower_blocks, coupling_blocks, precond_blocks, seg_blocks, links):
    cap, width = rhs.shape[1:]
    n_track, n_strip = lax.axis_size("track"), lax.axis_size("strip")
    track, strip = lax.axis_index("track"), lax.axis_index("strip")
    pos = jnp.stack([track, strip, seg_blocks[0]]).astype(jnp.int32)
    rhs = rhs[0]
    whole = n_track * n_strip
    chips = n_track // 2
    block = (cap, width)
    square = (width, width)
    stack = (cap, width, width)
    chunk = (whole, width // 128 + 2, 128)
    chain = (CHAINS, width)
    swap = [(i, i ^ 1) for i in range(n_track)]

    def flip(*stacks):
        kernel = functools.partial(flip_kernel, cap)
        return call(kernel, [(stack, jnp.bfloat16)] * len(stacks), [VMEM] * len(stacks), *stacks)

    maps, total, edge_map, local, ends, begins, through, last_two, lower, precond, diag, coupling = call(
        functools.partial(maps_kernel, cap),
        [stack, square, square, block, (2, width), chain, (CHAINS - 1,) + square, square] + [(stack, jnp.bfloat16)] * 4,
        [HBM] * 6 + [SMEM],
        rhs, links, lower_blocks[0], precond_blocks[0], principal_tiles[0], coupling_blocks[0], pos,
        scratch=[
            pltpu.VMEM(block, F32), pltpu.SMEM(links.shape, jnp.int32),
            pltpu.SemaphoreType.DMA((4 * CHAINS + 4,)),
        ],
    )
    other = lax.ppermute(total, "track", swap)
    lower_flip, precond_flip = flip(lower, precond)
    chip, send = call(
        functools.partial(pair_kernel, n_track),
        [square, chunk],
        [VMEM] * 3 + [SMEM] + [VMEM] * 6,
        total, other, ends, pos, maps, lower, lower_flip, precond_flip, diag, coupling,
    )
    nearer = []
    for k in range(1, chips - 1, 2):
        shifted = swap[:2]
        for i in range(2, n_track):
            shifted = shifted + [(i, 2 + (i - 2 + 2 * (k + i % 2)) % (n_track - 2))]
        nearer.append(lax.ppermute(chip, "track", shifted))

    state = image = rhs
    pairs = [(i, i ^ 1) for i in range(n_strip) if i ^ 1 < n_strip]
    cross = []
    for d in range(n_track):
        for i in range(n_strip):
            partner = i + 1 if i % 2 else i - 1
            if 0 <= partner < n_strip:
                cross.append((d * n_strip + i, d * n_strip + partner))
            else:
                cross.append((d * n_strip + i, (d ^ 1) * n_strip + i))
    for step_number in range(ITERS):
        recv = lax.all_to_all(send, ("strip", "track"), 0, 0)
        if step_number == 0:
            recv, diag, coupling, edge_map, *nearer = lax.optimization_barrier(
                (recv, diag, coupling, edge_map, *nearer)
            )
            edge_map = lax.ppermute(edge_map, "track", [((i + 1) % n_track, i) for i in range(n_track)])
            nearer += [lax.ppermute(part, "track", swap) for part in nearer]
            diag_flip, coupling_flip = flip(diag, coupling)
        value, first, second, entry = call(
            functools.partial(direction_kernel, cap, n_track),
            [block, block, block, (1, width)],
            [VMEM] * (7 + len(nearer)) + [SMEM],
            recv, local, begins, maps, through, other, coupling, *nearer, pos,
        )
        first = lax.ppermute(first, "strip", pairs)
        second = lax.ppermute(second, ("track", "strip"), cross)
        base, state, alpha = call(
            functools.partial(local_kernel, cap, step_number == 0),
            [block, (3,) + block, (1, width)],
            [VMEM] * 8 + [SMEM] * 2,
            value, entry, recv, state, image, diag_flip, lower, lower_flip, links, pos,
        )
        args = (
            base, first, second, value, recv, state, image, alpha, edge_map, coupling_flip, lower, lower_flip,
            precond_flip, maps, last_two, other, links, pos,
        )
        specs = [VMEM] * 16 + [SMEM] * 2
        if step_number < ITERS - 1:
            kernel = functools.partial(update_kernel, cap, n_track, n_strip, step_number == 0)
            image, local, begins, send = call(kernel, [block, block, chain, chunk], specs, *args)
        else:
            kernel = functools.partial(last_update_kernel, cap, n_track, n_strip)
            image, send = call(kernel, [block, (whole, 2, 128)], specs, *args)
    recv = lax.all_to_all(send, ("strip", "track"), 0, 0)
    solution, residual = call(final_kernel, [block, block], [VMEM] * 3, recv, state, image)
    return (solution[None], residual[None])


def solution(mesh):
    in_specs = (
        P("strip", "track", None),
        P("strip", "track", None, None),
        P("strip", "track", None, None),
        P("strip", "track", None, None),
        P("strip", "track", None, None),
        P("track"),
        P("strip", "track"),
    )
    out_specs = (P("strip", "track", None), P("strip", "track", None))
    return jax.shard_map(body, mesh=mesh, in_specs=in_specs, out_specs=out_specs, check_vma=False)
```

```python
import functools
import math

import jax
import jax.numpy as jnp
from jax import lax
from jax.experimental import pallas as pl
from jax.experimental.pallas import tpu as pltpu
from jax.sharding import PartitionSpec as P

ITERS = 6
CHAINS = 4
ROWS = 8
EARLY = 1
VMEM_BYTES = 16 * 1024 * 1024
PINNED = 1 << 19
NT = (((1,), (1,)), ((), ()))
NN = (((1,), (0,)), ((), ()))
VMEM = pl.BlockSpec(memory_space=pltpu.VMEM)
HBM = pl.BlockSpec(memory_space=pltpu.MemorySpace.HBM)
SMEM = pl.BlockSpec(memory_space=pltpu.SMEM)
F32 = jnp.float32


def pieces(value):
    high = value.astype(jnp.bfloat16)
    rest = value - high.astype(F32)
    middle = rest.astype(jnp.bfloat16)
    low = (rest - middle.astype(F32)).astype(jnp.bfloat16)
    return jnp.concatenate([high, middle, low], axis=0)


def split_row(row):
    return pieces(jnp.concatenate([row, row], axis=0))


def times(lhs, matrix, dims):
    out = lax.dot_general(lhs, matrix, dims, preferred_element_type=F32)
    return out[:ROWS] + out[2 * ROWS : 3 * ROWS] + out[4 * ROWS : 5 * ROWS]


def two_pieces(value):
    high = value.astype(jnp.bfloat16)
    return high, (value - high.astype(F32)).astype(jnp.bfloat16)


def times_matrix(value, matrix, dims):
    lhs = jnp.concatenate(two_pieces(value), axis=0)
    out = lax.dot_general(lhs, matrix, dims, preferred_element_type=F32)
    n = value.shape[0]
    return out[:n] + out[n:]


def product(left, right):
    high, rest = two_pieces(right)
    cross = lax.dot_general(left.astype(jnp.bfloat16), rest, NN, preferred_element_type=F32)
    return times_matrix(left, high, NN) + cross


def spread(row):
    return jnp.transpose(jnp.broadcast_to(row, (128, row.shape[1])))


def times_f32(column, matrix):
    wide = jnp.concatenate([column] * (matrix.shape[1] // 128), axis=1)
    return jnp.sum(matrix * wide, axis=0, keepdims=True)


def wide_row(ref, j):
    return jnp.broadcast_to(ref[j : j + 1, :], (ROWS, ref.shape[1]))


def is_live(pos_ref, j):
    return j < pos_ref[2]


def link(links_ref, pos_ref, j):
    joined = links_ref[0, j] if j else jnp.where(pos_ref[0] > 0, links_ref[0, 0], 0)
    return jnp.where(is_live(pos_ref, j), joined, 0).astype(F32)


def live_mask(pos_ref, shape):
    return lax.broadcasted_iota(jnp.int32, shape, 0) < pos_ref[2]


def dot_parts(residual, image):
    parts = []
    for left in (residual, image):
        partial = jnp.sum(left * image, axis=0, keepdims=True)
        parts.append(sum(partial[:, i : i + 128] for i in range(0, partial.shape[1], 128)))
    return parts


def halves(row):
    return [row[:, i : i + 128] for i in range(0, row.shape[1], 128)]


def send_ends(end, carried, first, dots, pos_ref, n_track, out_ref):
    track = pos_ref[0]
    carried = jnp.where(track % 2 == 0, carried, end)
    near = jnp.concatenate(halves(end) + dots, axis=0)
    far = jnp.concatenate(halves(carried) + dots, axis=0)
    back = jnp.concatenate(halves(first) + dots, axis=0)
    for i in range(out_ref.shape[0]):
        ahead = i % n_track - track
        out_ref[i] = jnp.where(ahead > 1, far, jnp.where(ahead == 1, near, back))


def chain_ends(state, maps_ref, last_two_ref, length):
    ends = [state[0][:1]]
    for q in range(1, CHAINS - 1):
        ends.append(state[q][:1] + times_f32(spread(ends[-1]), maps_ref[q * length + length - 1]))
    last = state[-1][:1] + times_f32(spread(state[-2][:1]), maps_ref[CHAINS * length - 1])
    ends.append(last + times_f32(spread(ends[-2]), last_two_ref[...]))
    return ends, last


def maps_kernel(
    cap, rhs_hbm, links_hbm, lower_hbm, precond_hbm, diag_hbm, coupling_hbm, pos_ref,
    maps_ref, total_ref, edge_ref, local_ref, ends_ref, begins_ref, through_ref, last_two_ref,
    lower_ref, precond_ref, diag_ref, coupling_ref,
    rhs_ref, links_ref, sems,
):
    width = lower_ref.shape[-1]
    length = cap // CHAINS
    copies = [
        pltpu.make_async_copy(rhs_hbm, rhs_ref, sems.at[0]),
        pltpu.make_async_copy(links_hbm, links_ref, sems.at[1]),
    ]

    def load(source, target, start, count):
        rows = pl.ds(start, count)
        copies.append(pltpu.make_async_copy(source.at[rows], target.at[rows], sems.at[len(copies)]))

    for begin, end in ((0, EARLY), (EARLY, length)):
        for source, target in ((lower_hbm, lower_ref), (precond_hbm, precond_ref)):
            for q in range(CHAINS):
                load(source, target, q * length + begin, end - begin)
    load(diag_hbm, diag_ref, 0, cap)
    load(coupling_hbm, coupling_ref, 0, cap)
    for copy in copies:
        copy.start()
    early = 2 + 2 * CHAINS
    for copy in copies[:early]:
        copy.wait()
    rows = lax.broadcasted_iota(jnp.int32, (width, width), 0)
    cols = lax.broadcasted_iota(jnp.int32, (width, width), 1)
    ident = jnp.where(rows == cols, 1.0, 0.0).astype(F32)
    state = [ident] * CHAINS
    local = [None] * CHAINS
    for t in range(length):
        if t == EARLY:
            for copy in copies[early:-2]:
                copy.wait()
        for q in range(CHAINS):
            j = q * length + t
            live, on = is_live(pos_ref, j), link(links_ref, pos_ref, j)
            if t == 0:
                inner = lax.dot_general(
                    ident.astype(jnp.bfloat16), lower_ref[j], NT, preferred_element_type=F32
                )
                value = lax.dot_general(
                    inner.astype(jnp.bfloat16), precond_ref[j], NT, preferred_element_type=F32
                )
            else:
                inner = times_matrix(state[q], lower_ref[j], NT)
                value = times_matrix(inner, precond_ref[j], NT)
            state[q] = jnp.where(live, -on * value, state[q])
            maps_ref[j] = state[q]
            inner = wide_row(rhs_ref, j)
            if t > 0:
                inner = inner - on * times(split_row(local[q]), lower_ref[j], NT)
            value = times(split_row(inner), precond_ref[j], NT)
            local[q] = jnp.where(live, value, local[q] if t > 0 else 0.0)
            local_ref[j : j + 1, :] = local[q][:1]
            if j == 0:
                edge_ref[...] = times_matrix(state[q], lower_ref[0], NN)
                ends_ref[1:2, :] = (on * times(split_row(local[q]), lower_ref[0], NN))[:1]
    span = 1
    while span < CHAINS:
        state = [
            state[q] if q < span else product(state[q - span], state[q])
            for q in range(CHAINS)
        ]
        if span == 1:
            last_two_ref[...] = state[-1]
        span *= 2
    for q in range(CHAINS - 1):
        through_ref[q] = state[q]
    total_ref[...] = state[-1]
    ends, _ = chain_ends(local, maps_ref, last_two_ref, length)
    ends_ref[0:1, :] = ends[-1]
    begins_ref[...] = jnp.concatenate(ends, axis=0)
    for copy in copies[-2:]:
        copy.wait()


def pair_kernel(n_track, total_ref, other_ref, ends_ref, last_two_ref, pos_ref, *refs):
    chip_ref, beyond_ref, send_ref = refs[-3:]
    first_core = pos_ref[0] % 2 == 0
    own, other = total_ref[...], other_ref[...]
    early, late = jnp.where(first_core, own, other), jnp.where(first_core, other, own)
    chip_ref[...] = product(early, late)
    dots = [jnp.zeros((1, 128), F32)] * 2
    end = ends_ref[0:1, :]
    carried = times_f32(spread(end), other_ref[...])
    send_ends(end, carried, ends_ref[1:2, :], dots, pos_ref, n_track, send_ref)
    beyond_ref[...] = product(last_two_ref[...], other_ref[...])


def direction_kernel(cap, n_track, recv_ref, local_ref, begins_ref, maps_ref, through_ref, other_ref, coupling_ref, *refs):
    chip_refs, (pos_ref, value_ref, first_ref, second_ref, entry_ref) = refs[:-5], refs[-5:]
    track, strip = pos_ref[0], pos_ref[1]
    width = local_ref.shape[1]
    length = cap // CHAINS
    half = width // 128
    base = strip * n_track if recv_ref.shape[0] > n_track else 0
    chip = track // 2

    def chunk(index, valid):
        got = recv_ref[base + jnp.clip(index, 0, n_track - 1)]
        got = jnp.where(valid, got, 0.0)
        return jnp.concatenate([got[h : h + 1] for h in range(half)], axis=1)

    def chip_end(i):
        valid = chip - i >= 0
        return chunk(2 * (chip - i), valid) + chunk(2 * (chip - i) + 1, valid)

    def chip_map(i):
        mine, paired = chip_refs[i // 2][...], chip_refs[i // 2 + len(chip_refs) // 2][...]
        return jnp.where(track % 2 == i % 2, mine, paired)

    furthest = n_track // 2 - 1
    entry = chip_end(furthest)
    for i in range(furthest - 1, 0, -1):
        entry = chip_end(i) + times_f32(spread(entry), chip_map(i - 1))
    inside = chunk(track - 1, track > 0) + times_f32(spread(entry), other_ref[...])
    entry = jnp.where(track % 2 == 1, inside, entry)
    entry_ref[...] = entry
    columns = [spread(entry)]
    for q in range(1, CHAINS):
        begin = begins_ref[q - 1 : q, :] + times_f32(columns[0], through_ref[q - 1])
        columns.append(spread(begin))
    even = strip % 2 == 0
    for j in range(cap):
        value = local_ref[j : j + 1, :] + times_f32(columns[j // length], maps_ref[j])
        masked = jnp.where(is_live(pos_ref, j), value, 0.0)
        value_ref[j : j + 1, :] = masked
        crossed = times(split_row(jnp.broadcast_to(masked, (ROWS, width))), coupling_ref[j], NN)[:1]
        first_ref[j : j + 1, :] = jnp.where(even, masked, crossed)
        second_ref[j : j + 1, :] = jnp.where(even, crossed, masked)


def flip_kernel(cap, *refs):
    sources, targets = refs[: len(refs) // 2], refs[len(refs) // 2 :]
    for source, target in zip(sources, targets):
        for j in range(cap):
            target[j] = jnp.transpose(source[j])


def alpha_of(recv_ref):
    total = jnp.sum(recv_ref[...], axis=0)
    inner = jnp.sum(total[-2:-1], axis=1, keepdims=True)
    energy = jnp.sum(total[-1:], axis=1, keepdims=True)
    return inner / (energy + 1e-6)


def local_kernel(
    cap, first, value_ref, entry_ref, recv_ref, state_ref, image_ref, diag_ref, lower_ref,
    lower_flip_ref, links_ref, pos_ref, base_ref, next_ref, alpha_ref,
):
    width = value_ref.shape[1]
    on = [link(links_ref, pos_ref, j) for j in range(cap)]
    lowered = on[0] * times(split_row(wide_row(entry_ref, 0)), lower_flip_ref[0], NN)
    held = None
    for j in range(cap):
        lhs = split_row(wide_row(value_ref, j))
        own = times(lhs, diag_ref[j], NT) + lowered
        if j > 0:
            held = held + on[j] * times(lhs, lower_ref[j], NN)
            base_ref[j - 1 : j, :] = held[:1]
        if j < cap - 1:
            lowered = on[j + 1] * times(lhs, lower_flip_ref[j + 1], NN)
        held = own
    base_ref[cap - 1 : cap, :] = held[:1]
    if first:
        next_ref[0] = jnp.where(live_mask(pos_ref, (cap, width)), state_ref[...], 0.0)
        next_ref[1] = value_ref[...]
        next_ref[2] = jnp.zeros_like(value_ref[...])
        alpha_ref[...] = jnp.zeros((1, width), F32)
    else:
        alpha = alpha_of(recv_ref)
        next_ref[0] = state_ref[0] - alpha * image_ref[...]
        next_ref[1] = state_ref[1] - alpha * value_ref[...]
        next_ref[2] = state_ref[2] + alpha * state_ref[1]
        alpha_ref[...] = jnp.broadcast_to(alpha, (1, width))


def update_kernel(
    cap, n_track, n_strip, first, base_ref, first_ref, second_ref, value_ref, recv_ref, state_ref, image_ref, alpha_ref,
    edge_map_ref, coupling_flip_ref, lower_ref, lower_flip_ref, precond_flip_ref, maps_ref, last_two_ref, beyond_ref, other_ref, links_ref, pos_ref,
    next_ref, local_ref, begins_ref, send_ref,
):
    track, strip, count = pos_ref[0], pos_ref[1], pos_ref[2]
    width = base_ref.shape[1]
    length = cap // CHAINS
    odd = strip % 2 == 1
    one, two = first_ref[...], second_ref[...]
    below = jnp.where(strip > 0, jnp.where(odd, one, two), 0.0)
    above = jnp.where(strip < n_strip - 1, jnp.where(odd, two, one), 0.0)
    base = strip * n_track if recv_ref.shape[0] > n_track else 0
    ahead = recv_ref[base + jnp.minimum(track + 1, n_track - 1)]
    ahead = jnp.concatenate([ahead[h : h + 1] for h in range(width // 128)], axis=1)
    ahead = ahead + times_f32(spread(value_ref[pl.ds(count - 1, 1), :]), edge_map_ref[...])
    ahead = jnp.where(track < n_track - 1, ahead, 0.0)
    at_end = lax.broadcasted_iota(jnp.int32, (cap, width), 0) == count - 1
    known = base_ref[...] + above + jnp.where(at_end, ahead, 0.0)
    alpha = wide_row(alpha_ref, 0)

    def image_row(j):
        row = wide_row(known, j) + times(split_row(wide_row(below, j)), coupling_flip_ref[j], NN)
        row = jnp.where(is_live(pos_ref, j), row, 0.0)
        row = row if first else wide_row(image_ref, j) - alpha * row
        next_ref[j : j + 1, :] = row[:1]
        return row

    state = [None] * CHAINS
    rows = [image_row(q * length) for q in range(CHAINS)]
    for t in range(length):
        if local_ref is not None and t > 0:
            for q in range(CHAINS):
                j = q * length + t
                lowered = times(split_row(state[q]), lower_flip_ref[j], NN)
                rows[q] = rows[q] - link(links_ref, pos_ref, j) * lowered
        later = [image_row(q * length + t + 1) for q in range(CHAINS)] if t + 1 < length else []
        for q in range(0 if local_ref is None else CHAINS):
            j = q * length + t
            value = times(split_row(rows[q]), precond_flip_ref[j], NN)
            state[q] = jnp.where(is_live(pos_ref, j), value, state[q] if t > 0 else 0.0)
            local_ref[j : j + 1, :] = state[q][:1]
            if j == 0:
                edge = link(links_ref, pos_ref, 0) * times(split_row(state[q]), lower_ref[0], NN)
        rows = later
    dots = dot_parts(state_ref[0], next_ref[...])
    if local_ref is None:
        packed = jnp.concatenate(dots, axis=0)
        for i in range(send_ref.shape[0]):
            send_ref[i] = packed
        return
    ends, last = chain_ends(state, maps_ref, last_two_ref, length)
    begins_ref[...] = jnp.concatenate(ends, axis=0)
    carried = times_f32(spread(last), other_ref[...]) + times_f32(spread(ends[-3]), beyond_ref[...])
    send_ends(ends[-1], carried, edge[:1], dots, pos_ref, n_track, send_ref)


def last_update_kernel(cap, n_track, n_strip, *refs):
    update_kernel(cap, n_track, n_strip, False, *refs[:-1], None, None, refs[-1])


def final_kernel(recv_ref, state_ref, image_ref, solution_ref, residual_ref):
    alpha = alpha_of(recv_ref)
    solution_ref[...] = state_ref[2] + alpha * state_ref[1]
    residual_ref[...] = state_ref[0] - alpha * image_ref[...]


def call(kernel, outs, specs, *args, scratch=(), vmem=VMEM_BYTES):
    outs = [out if len(out) == 2 and isinstance(out[0], tuple) else (out, F32) for out in outs]
    args = [
        pltpu.with_memory_space_constraint(arg, spec.memory_space) if arg.size >= PINNED or spec is HBM else arg
        for arg, spec in zip(args, specs)
    ]
    return pl.pallas_call(
        kernel,
        out_shape=[
            pltpu.VMEM(shape, dtype) if math.prod(shape) >= PINNED else jax.ShapeDtypeStruct(shape, dtype)
            for shape, dtype in outs
        ],
        in_specs=specs,
        out_specs=[VMEM] * len(outs),
        scratch_shapes=scratch,
        compiler_params=pltpu.CompilerParams(vmem_limit_bytes=vmem),
    )(*args)


def body(rhs, principal_tiles, lower_blocks, coupling_blocks, precond_blocks, seg_blocks, links):
    cap, width = rhs.shape[1:]
    n_track, n_strip = lax.axis_size("track"), lax.axis_size("strip")
    track, strip = lax.axis_index("track"), lax.axis_index("strip")
    pos = jnp.stack([track, strip, seg_blocks[0]]).astype(jnp.int32)
    rhs = rhs[0]
    whole = n_track * n_strip
    chips = n_track // 2
    block = (cap, width)
    square = (width, width)
    stack = (cap, width, width)
    chunk = (whole, width // 128 + 2, 128)
    chain = (CHAINS, width)
    swap = [(i, i ^ 1) for i in range(n_track)]

    def flip(*stacks):
        kernel = functools.partial(flip_kernel, cap)
        return call(kernel, [(stack, jnp.bfloat16)] * len(stacks), [VMEM] * len(stacks), *stacks)

    maps, total, edge_map, local, ends, begins, through, last_two, lower, precond, diag, coupling = call(
        functools.partial(maps_kernel, cap),
        [stack, square, square, block, (2, width), chain, (CHAINS - 1,) + square, square] + [(stack, jnp.bfloat16)] * 4,
        [HBM] * 6 + [SMEM],
        rhs, links, lower_blocks[0], precond_blocks[0], principal_tiles[0], coupling_blocks[0], pos,
        scratch=[
            pltpu.VMEM(block, F32), pltpu.SMEM(links.shape, jnp.int32),
            pltpu.SemaphoreType.DMA((4 * CHAINS + 4,)),
        ],
    )
    other = lax.ppermute(total, "track", swap)
    lower_flip, precond_flip = flip(lower, precond)
    chip, beyond, send = call(
        functools.partial(pair_kernel, n_track),
        [square, square, (n_track,) + chunk[1:]],
        [VMEM] * 4 + [SMEM] + [VMEM] * 6,
        total, other, ends, last_two, pos, maps, lower, lower_flip, precond_flip, diag, coupling,
    )
    nearer = []
    for k in range(1, chips - 1, 2):
        shifted = swap[:2]
        for i in range(2, n_track):
            shifted = shifted + [(i, 2 + (i - 2 + 2 * (k + i % 2)) % (n_track - 2))]
        nearer.append(lax.ppermute(chip, "track", shifted))

    state = image = rhs
    pairs = [(i, i ^ 1) for i in range(n_strip) if i ^ 1 < n_strip]
    cross = []
    for d in range(n_track):
        for i in range(n_strip):
            partner = i + 1 if i % 2 else i - 1
            if 0 <= partner < n_strip:
                cross.append((d * n_strip + i, d * n_strip + partner))
            else:
                cross.append((d * n_strip + i, (d ^ 1) * n_strip + i))
    for step_number in range(ITERS):
        recv = lax.all_to_all(send, ("strip", "track") if step_number else "track", 0, 0)
        if step_number == 0:
            recv, edge_map, coupling, *nearer = lax.optimization_barrier((recv, edge_map, coupling, *nearer))
            coupling_flip, = flip(coupling)
            edge_map = lax.ppermute(edge_map, "track", [((i + 1) % n_track, i) for i in range(n_track)])
            nearer += [lax.ppermute(part, "track", swap) for part in nearer]
        value, first, second, entry = call(
            functools.partial(direction_kernel, cap, n_track),
            [block, block, block, (1, width)],
            [VMEM] * (7 + len(nearer)) + [SMEM],
            recv, local, begins, maps, through, other, coupling, *nearer, pos,
        )
        first = lax.ppermute(first, "strip", pairs)
        second = lax.ppermute(second, ("track", "strip"), cross)
        base, state, alpha = call(
            functools.partial(local_kernel, cap, step_number == 0),
            [block, (3,) + block, (1, width)],
            [VMEM] * 8 + [SMEM] * 2,
            value, entry, recv, state, image, diag, lower, lower_flip, links, pos,
        )
        args = (
            base, first, second, value, recv, state, image, alpha, edge_map, coupling_flip, lower, lower_flip,
            precond_flip, maps, last_two, beyond, other, links, pos,
        )
        specs = [VMEM] * 17 + [SMEM] * 2
        if step_number < ITERS - 1:
            kernel = functools.partial(update_kernel, cap, n_track, n_strip, step_number == 0)
            image, local, begins, send = call(kernel, [block, block, chain, chunk], specs, *args)
        else:
            kernel = functools.partial(last_update_kernel, cap, n_track, n_strip)
            image, send = call(kernel, [block, (whole, 2, 128)], specs, *args)
    recv = lax.all_to_all(send, ("strip", "track"), 0, 0)
    solution, residual = call(final_kernel, [block, block], [VMEM] * 3, recv, state, image)
    return (solution[None], residual[None])


def solution(mesh):
    in_specs = (
        P("strip", "track", None),
        P("strip", "track", None, None),
        P("strip", "track", None, None),
        P("strip", "track", None, None),
        P("strip", "track", None, None),
        P("track"),
        P("strip", "track"),
    )
    out_specs = (P("strip", "track", None), P("strip", "track", None))
    return jax.shard_map(body, mesh=mesh, in_specs=in_specs, out_specs=out_specs, check_vma=False)
```

```python
import functools
import math

import jax
import jax.numpy as jnp
from jax import lax
from jax.experimental import pallas as pl
from jax.experimental.pallas import tpu as pltpu
from jax.sharding import PartitionSpec as P

ITERS = 6
CHAINS = 4
ROWS = 8
EARLY = 1
VMEM_BYTES = 16 * 1024 * 1024
PINNED = 1 << 19
NT = (((1,), (1,)), ((), ()))
NN = (((1,), (0,)), ((), ()))
VMEM = pl.BlockSpec(memory_space=pltpu.VMEM)
HBM = pl.BlockSpec(memory_space=pltpu.MemorySpace.HBM)
SMEM = pl.BlockSpec(memory_space=pltpu.SMEM)
F32 = jnp.float32


def pieces(value):
    high = value.astype(jnp.bfloat16)
    rest = value - high.astype(F32)
    middle = rest.astype(jnp.bfloat16)
    low = (rest - middle.astype(F32)).astype(jnp.bfloat16)
    return jnp.concatenate([high, middle, low], axis=0)


def split_row(row):
    return pieces(jnp.concatenate([row, row], axis=0))


def times(lhs, matrix, dims):
    out = lax.dot_general(lhs, matrix, dims, preferred_element_type=F32)
    return out[:ROWS] + out[2 * ROWS : 3 * ROWS] + out[4 * ROWS : 5 * ROWS]


def two_pieces(value):
    high = value.astype(jnp.bfloat16)
    return high, (value - high.astype(F32)).astype(jnp.bfloat16)


def times_matrix(value, matrix, dims):
    lhs = jnp.concatenate(two_pieces(value), axis=0)
    out = lax.dot_general(lhs, matrix, dims, preferred_element_type=F32)
    n = value.shape[0]
    return out[:n] + out[n:]


def product(left, right):
    high, rest = two_pieces(right)
    cross = lax.dot_general(left.astype(jnp.bfloat16), rest, NN, preferred_element_type=F32)
    return times_matrix(left, high, NN) + cross


def spread(row):
    return jnp.transpose(jnp.broadcast_to(row, (128, row.shape[1])))


def times_f32(column, matrix):
    wide = jnp.concatenate([column] * (matrix.shape[1] // 128), axis=1)
    return jnp.sum(matrix * wide, axis=0, keepdims=True)


def wide_row(ref, j):
    return jnp.broadcast_to(ref[j : j + 1, :], (ROWS, ref.shape[1]))


def is_live(pos_ref, j):
    return j < pos_ref[2]


def link(links_ref, pos_ref, j):
    joined = links_ref[0, j] if j else jnp.where(pos_ref[0] > 0, links_ref[0, 0], 0)
    return jnp.where(is_live(pos_ref, j), joined, 0).astype(F32)


def live_mask(pos_ref, shape):
    return lax.broadcasted_iota(jnp.int32, shape, 0) < pos_ref[2]


def dot_parts(residual, image):
    parts = []
    for left in (residual, image):
        partial = jnp.sum(left * image, axis=0, keepdims=True)
        parts.append(sum(partial[:, i : i + 128] for i in range(0, partial.shape[1], 128)))
    return parts


def halves(row):
    return [row[:, i : i + 128] for i in range(0, row.shape[1], 128)]


def send_ends(end, carried, first, dots, pos_ref, n_track, out_ref):
    track = pos_ref[0]
    carried = jnp.where(track % 2 == 0, carried, end)
    near = jnp.concatenate(halves(end) + dots, axis=0)
    far = jnp.concatenate(halves(carried) + dots, axis=0)
    back = jnp.concatenate(halves(first) + dots, axis=0)
    for i in range(out_ref.shape[0]):
        ahead = i % n_track - track
        out_ref[i] = jnp.where(ahead > 1, far, jnp.where(ahead == 1, near, back))


def chain_ends(state, maps_ref, last_two_ref, length):
    ends = [state[0][:1]]
    for q in range(1, CHAINS - 1):
        ends.append(state[q][:1] + times_f32(spread(ends[-1]), maps_ref[q * length + length - 1]))
    last = state[-1][:1] + times_f32(spread(state[-2][:1]), maps_ref[CHAINS * length - 1])
    ends.append(last + times_f32(spread(ends[-2]), last_two_ref[...]))
    return ends, last


def maps_kernel(
    cap, rhs_hbm, links_hbm, lower_hbm, precond_hbm, diag_hbm, coupling_hbm, pos_ref,
    maps_ref, total_ref, edge_ref, local_ref, ends_ref, begins_ref, through_ref, last_two_ref,
    lower_ref, precond_ref, diag_ref, coupling_ref,
    rhs_ref, links_ref, sems,
):
    width = lower_ref.shape[-1]
    length = cap // CHAINS
    copies = [
        pltpu.make_async_copy(rhs_hbm, rhs_ref, sems.at[0]),
        pltpu.make_async_copy(links_hbm, links_ref, sems.at[1]),
    ]

    def load(source, target, start, count):
        rows = pl.ds(start, count)
        copies.append(pltpu.make_async_copy(source.at[rows], target.at[rows], sems.at[len(copies)]))

    for begin, end in ((0, EARLY), (EARLY, length)):
        for source, target in ((lower_hbm, lower_ref), (precond_hbm, precond_ref)):
            for q in range(CHAINS):
                load(source, target, q * length + begin, end - begin)
    load(diag_hbm, diag_ref, 0, cap)
    load(coupling_hbm, coupling_ref, 0, cap)
    for copy in copies:
        copy.start()
    early = 2 + 2 * CHAINS
    for copy in copies[:early]:
        copy.wait()
    rows = lax.broadcasted_iota(jnp.int32, (width, width), 0)
    cols = lax.broadcasted_iota(jnp.int32, (width, width), 1)
    ident = jnp.where(rows == cols, 1.0, 0.0).astype(F32)
    state = [ident] * CHAINS
    local = [None] * CHAINS
    for t in range(length):
        if t == EARLY:
            for copy in copies[early:-2]:
                copy.wait()
        for q in range(CHAINS):
            j = q * length + t
            live, on = is_live(pos_ref, j), link(links_ref, pos_ref, j)
            if t == 0:
                inner = lax.dot_general(
                    ident.astype(jnp.bfloat16), lower_ref[j], NT, preferred_element_type=F32
                )
                value = lax.dot_general(
                    inner.astype(jnp.bfloat16), precond_ref[j], NT, preferred_element_type=F32
                )
            else:
                inner = times_matrix(state[q], lower_ref[j], NT)
                value = times_matrix(inner, precond_ref[j], NT)
            state[q] = jnp.where(live, -on * value, state[q])
            maps_ref[j] = state[q]
            inner = wide_row(rhs_ref, j)
            if t > 0:
                inner = inner - on * times(split_row(local[q]), lower_ref[j], NT)
            value = times(split_row(inner), precond_ref[j], NT)
            local[q] = jnp.where(live, value, local[q] if t > 0 else 0.0)
            local_ref[j : j + 1, :] = local[q][:1]
            if j == 0:
                edge_ref[...] = times_matrix(state[q], lower_ref[0], NN)
                ends_ref[1:2, :] = (on * times(split_row(local[q]), lower_ref[0], NN))[:1]
    span = 1
    while span < CHAINS:
        state = [
            state[q] if q < span else product(state[q - span], state[q])
            for q in range(CHAINS)
        ]
        if span == 1:
            last_two_ref[...] = state[-1]
        span *= 2
    for q in range(CHAINS - 1):
        through_ref[q] = state[q]
    total_ref[...] = state[-1]
    ends, _ = chain_ends(local, maps_ref, last_two_ref, length)
    ends_ref[0:1, :] = ends[-1]
    begins_ref[...] = jnp.concatenate(ends, axis=0)
    for copy in copies[-2:]:
        copy.wait()


def pair_kernel(n_track, total_ref, other_ref, ends_ref, last_two_ref, pos_ref, *refs):
    chip_ref, beyond_ref, send_ref = refs[-3:]
    first_core = pos_ref[0] % 2 == 0
    own, other = total_ref[...], other_ref[...]
    early, late = jnp.where(first_core, own, other), jnp.where(first_core, other, own)
    chip_ref[...] = product(early, late)
    dots = [jnp.zeros((1, 128), F32)] * 2
    end = ends_ref[0:1, :]
    carried = times_f32(spread(end), other_ref[...])
    send_ends(end, carried, ends_ref[1:2, :], dots, pos_ref, n_track, send_ref)
    beyond_ref[...] = product(last_two_ref[...], other_ref[...])


def chip_map(chip_refs, pos_ref, i):
    mine, paired = chip_refs[i // 2][...], chip_refs[i // 2 + len(chip_refs) // 2][...]
    return jnp.where(pos_ref[0] % 2 == i % 2, mine, paired)


def fold_kernel(cap, chips, coupling_ref, other_ref, pos_ref, *refs):
    chip_refs, (flip_ref, *out_refs) = refs[: chips - 2], refs[chips - 2 :]
    flip_kernel(cap, coupling_ref, flip_ref)
    value = None
    for i, out_ref in enumerate(out_refs):
        nearer = chip_map(chip_refs, pos_ref, i)
        if value is None:
            value = jnp.where(pos_ref[0] % 2 == 1, product(nearer, other_ref[...]), nearer)
        else:
            value = product(nearer, value)
        out_ref[...] = value


def direction_kernel(cap, n_track, folded, recv_ref, local_ref, begins_ref, maps_ref, through_ref, other_ref, coupling_ref, *refs):
    chip_refs, (pos_ref, value_ref, first_ref, second_ref, entry_ref) = refs[:-5], refs[-5:]
    track, strip = pos_ref[0], pos_ref[1]
    width = local_ref.shape[1]
    length = cap // CHAINS
    half = width // 128
    base = strip * n_track if recv_ref.shape[0] > n_track else 0
    chip = track // 2

    def chunk(index, valid):
        got = recv_ref[base + jnp.clip(index, 0, n_track - 1)]
        got = jnp.where(valid, got, 0.0)
        return jnp.concatenate([got[h : h + 1] for h in range(half)], axis=1)

    def chip_end(i):
        valid = chip - i >= 0
        return chunk(2 * (chip - i), valid) + chunk(2 * (chip - i) + 1, valid)

    furthest = n_track // 2 - 1
    if folded:
        entry = chip_end(1)
        inside = chunk(track - 1, track > 0) + times_f32(spread(entry), other_ref[...])
        entry = jnp.where(track % 2 == 1, inside, entry)
        for i in range(2, furthest + 1):
            entry = entry + times_f32(spread(chip_end(i)), chip_refs[i - 2][...])
    else:
        entry = chip_end(furthest)
        for i in range(furthest - 1, 0, -1):
            entry = chip_end(i) + times_f32(spread(entry), chip_map(chip_refs, pos_ref, i - 1))
        inside = chunk(track - 1, track > 0) + times_f32(spread(entry), other_ref[...])
        entry = jnp.where(track % 2 == 1, inside, entry)
    entry_ref[...] = entry
    columns = [spread(entry)]
    for q in range(1, CHAINS):
        begin = begins_ref[q - 1 : q, :] + times_f32(columns[0], through_ref[q - 1])
        columns.append(spread(begin))
    even = strip % 2 == 0
    for j in range(cap):
        value = local_ref[j : j + 1, :] + times_f32(columns[j // length], maps_ref[j])
        masked = jnp.where(is_live(pos_ref, j), value, 0.0)
        value_ref[j : j + 1, :] = masked
        crossed = times(split_row(jnp.broadcast_to(masked, (ROWS, width))), coupling_ref[j], NN)[:1]
        first_ref[j : j + 1, :] = jnp.where(even, masked, crossed)
        second_ref[j : j + 1, :] = jnp.where(even, crossed, masked)


def flip_kernel(cap, *refs):
    sources, targets = refs[: len(refs) // 2], refs[len(refs) // 2 :]
    for source, target in zip(sources, targets):
        for j in range(cap):
            target[j] = jnp.transpose(source[j])


def alpha_of(recv_ref):
    total = jnp.sum(recv_ref[...], axis=0)
    inner = jnp.sum(total[-2:-1], axis=1, keepdims=True)
    energy = jnp.sum(total[-1:], axis=1, keepdims=True)
    return inner / (energy + 1e-6)


def local_kernel(
    cap, first, value_ref, entry_ref, recv_ref, state_ref, image_ref, diag_ref, lower_ref,
    lower_flip_ref, links_ref, pos_ref, base_ref, next_ref, alpha_ref,
):
    width = value_ref.shape[1]
    on = [link(links_ref, pos_ref, j) for j in range(cap)]
    lowered = on[0] * times(split_row(wide_row(entry_ref, 0)), lower_flip_ref[0], NN)
    held = None
    for j in range(cap):
        lhs = split_row(wide_row(value_ref, j))
        own = times(lhs, diag_ref[j], NT) + lowered
        if j > 0:
            held = held + on[j] * times(lhs, lower_ref[j], NN)
            base_ref[j - 1 : j, :] = held[:1]
        if j < cap - 1:
            lowered = on[j + 1] * times(lhs, lower_flip_ref[j + 1], NN)
        held = own
    base_ref[cap - 1 : cap, :] = held[:1]
    if first:
        next_ref[0] = jnp.where(live_mask(pos_ref, (cap, width)), state_ref[...], 0.0)
        next_ref[1] = value_ref[...]
        next_ref[2] = jnp.zeros_like(value_ref[...])
        alpha_ref[...] = jnp.zeros((1, width), F32)
    else:
        alpha = alpha_of(recv_ref)
        next_ref[0] = state_ref[0] - alpha * image_ref[...]
        next_ref[1] = state_ref[1] - alpha * value_ref[...]
        next_ref[2] = state_ref[2] + alpha * state_ref[1]
        alpha_ref[...] = jnp.broadcast_to(alpha, (1, width))


def update_kernel(
    cap, n_track, n_strip, first, base_ref, first_ref, second_ref, value_ref, recv_ref, state_ref, image_ref, alpha_ref,
    edge_map_ref, coupling_flip_ref, lower_ref, lower_flip_ref, precond_flip_ref, maps_ref, last_two_ref, beyond_ref, other_ref, links_ref, pos_ref,
    next_ref, local_ref, begins_ref, send_ref,
):
    track, strip, count = pos_ref[0], pos_ref[1], pos_ref[2]
    width = base_ref.shape[1]
    length = cap // CHAINS
    odd = strip % 2 == 1
    one, two = first_ref[...], second_ref[...]
    below = jnp.where(strip > 0, jnp.where(odd, one, two), 0.0)
    above = jnp.where(strip < n_strip - 1, jnp.where(odd, two, one), 0.0)
    base = strip * n_track if recv_ref.shape[0] > n_track else 0
    ahead = recv_ref[base + jnp.minimum(track + 1, n_track - 1)]
    ahead = jnp.concatenate([ahead[h : h + 1] for h in range(width // 128)], axis=1)
    ahead = ahead + times_f32(spread(value_ref[pl.ds(count - 1, 1), :]), edge_map_ref[...])
    ahead = jnp.where(track < n_track - 1, ahead, 0.0)
    at_end = lax.broadcasted_iota(jnp.int32, (cap, width), 0) == count - 1
    known = base_ref[...] + above + jnp.where(at_end, ahead, 0.0)
    alpha = wide_row(alpha_ref, 0)

    def image_row(j):
        row = wide_row(known, j) + times(split_row(wide_row(below, j)), coupling_flip_ref[j], NN)
        row = jnp.where(is_live(pos_ref, j), row, 0.0)
        row = row if first else wide_row(image_ref, j) - alpha * row
        next_ref[j : j + 1, :] = row[:1]
        return row

    state = [None] * CHAINS
    rows = [image_row(q * length) for q in range(CHAINS)]
    for t in range(length):
        if local_ref is not None and t > 0:
            for q in range(CHAINS):
                j = q * length + t
                lowered = times(split_row(state[q]), lower_flip_ref[j], NN)
                rows[q] = rows[q] - link(links_ref, pos_ref, j) * lowered
        later = [image_row(q * length + t + 1) for q in range(CHAINS)] if t + 1 < length else []
        for q in range(0 if local_ref is None else CHAINS):
            j = q * length + t
            value = times(split_row(rows[q]), precond_flip_ref[j], NN)
            state[q] = jnp.where(is_live(pos_ref, j), value, state[q] if t > 0 else 0.0)
            local_ref[j : j + 1, :] = state[q][:1]
            if j == 0:
                edge = link(links_ref, pos_ref, 0) * times(split_row(state[q]), lower_ref[0], NN)
        rows = later
    dots = dot_parts(state_ref[0], next_ref[...])
    if local_ref is None:
        packed = jnp.concatenate(dots, axis=0)
        for i in range(send_ref.shape[0]):
            send_ref[i] = packed
        return
    ends, last = chain_ends(state, maps_ref, last_two_ref, length)
    begins_ref[...] = jnp.concatenate(ends, axis=0)
    carried = times_f32(spread(last), other_ref[...]) + times_f32(spread(ends[-3]), beyond_ref[...])
    send_ends(ends[-1], carried, edge[:1], dots, pos_ref, n_track, send_ref)


def last_update_kernel(cap, n_track, n_strip, *refs):
    update_kernel(cap, n_track, n_strip, False, *refs[:-1], None, None, refs[-1])


def final_kernel(recv_ref, state_ref, image_ref, solution_ref, residual_ref):
    alpha = alpha_of(recv_ref)
    solution_ref[...] = state_ref[2] + alpha * state_ref[1]
    residual_ref[...] = state_ref[0] - alpha * image_ref[...]


def call(kernel, outs, specs, *args, scratch=(), vmem=VMEM_BYTES):
    outs = [out if len(out) == 2 and isinstance(out[0], tuple) else (out, F32) for out in outs]
    args = [
        pltpu.with_memory_space_constraint(arg, spec.memory_space) if arg.size >= PINNED or spec is HBM else arg
        for arg, spec in zip(args, specs)
    ]
    return pl.pallas_call(
        kernel,
        out_shape=[
            pltpu.VMEM(shape, dtype) if math.prod(shape) >= PINNED else jax.ShapeDtypeStruct(shape, dtype)
            for shape, dtype in outs
        ],
        in_specs=specs,
        out_specs=[VMEM] * len(outs),
        scratch_shapes=scratch,
        compiler_params=pltpu.CompilerParams(vmem_limit_bytes=vmem),
    )(*args)


def body(rhs, principal_tiles, lower_blocks, coupling_blocks, precond_blocks, seg_blocks, links):
    cap, width = rhs.shape[1:]
    n_track, n_strip = lax.axis_size("track"), lax.axis_size("strip")
    track, strip = lax.axis_index("track"), lax.axis_index("strip")
    pos = jnp.stack([track, strip, seg_blocks[0]]).astype(jnp.int32)
    rhs = rhs[0]
    whole = n_track * n_strip
    chips = n_track // 2
    block = (cap, width)
    square = (width, width)
    stack = (cap, width, width)
    chunk = (whole, width // 128 + 2, 128)
    chain = (CHAINS, width)
    swap = [(i, i ^ 1) for i in range(n_track)]

    def flip(*stacks):
        kernel = functools.partial(flip_kernel, cap)
        return call(kernel, [(stack, jnp.bfloat16)] * len(stacks), [VMEM] * len(stacks), *stacks)

    maps, total, edge_map, local, ends, begins, through, last_two, lower, precond, diag, coupling = call(
        functools.partial(maps_kernel, cap),
        [stack, square, square, block, (2, width), chain, (CHAINS - 1,) + square, square] + [(stack, jnp.bfloat16)] * 4,
        [HBM] * 6 + [SMEM],
        rhs, links, lower_blocks[0], precond_blocks[0], principal_tiles[0], coupling_blocks[0], pos,
        scratch=[
            pltpu.VMEM(block, F32), pltpu.SMEM(links.shape, jnp.int32),
            pltpu.SemaphoreType.DMA((4 * CHAINS + 4,)),
        ],
    )
    other = lax.ppermute(total, "track", swap)
    lower_flip, precond_flip = flip(lower, precond)
    chip, beyond, send = call(
        functools.partial(pair_kernel, n_track),
        [square, square, (n_track,) + chunk[1:]],
        [VMEM] * 4 + [SMEM] + [VMEM] * 6,
        total, other, ends, last_two, pos, maps, lower, lower_flip, precond_flip, diag, coupling,
    )
    nearer = []
    for k in range(1, chips - 1, 2):
        shifted = swap[:2]
        for i in range(2, n_track):
            shifted = shifted + [(i, 2 + (i - 2 + 2 * (k + i % 2)) % (n_track - 2))]
        nearer.append(lax.ppermute(chip, "track", shifted))

    state = image = rhs
    pairs = [(i, i ^ 1) for i in range(n_strip) if i ^ 1 < n_strip]
    cross = []
    for d in range(n_track):
        for i in range(n_strip):
            partner = i + 1 if i % 2 else i - 1
            if 0 <= partner < n_strip:
                cross.append((d * n_strip + i, d * n_strip + partner))
            else:
                cross.append((d * n_strip + i, (d ^ 1) * n_strip + i))
    for step_number in range(ITERS):
        recv = lax.all_to_all(send, ("strip", "track") if step_number else "track", 0, 0)
        if step_number == 0:
            recv, edge_map, coupling, *nearer = lax.optimization_barrier((recv, edge_map, coupling, *nearer))
            edge_map = lax.ppermute(edge_map, "track", [((i + 1) % n_track, i) for i in range(n_track)])
            nearer += [lax.ppermute(part, "track", swap) for part in nearer]
        value, first, second, entry = call(
            functools.partial(direction_kernel, cap, n_track, step_number > 0),
            [block, block, block, (1, width)],
            [VMEM] * (7 + len(nearer)) + [SMEM],
            recv, local, begins, maps, through, other, coupling, *nearer, pos,
        )
        if step_number == 0:
            coupling_flip, *nearer = call(
                functools.partial(fold_kernel, cap, chips),
                [(stack, jnp.bfloat16)] + [square] * (chips - 2),
                [VMEM] * 2 + [SMEM] + [VMEM] * len(nearer),
                coupling, other, pos, *nearer,
            )
        first = lax.ppermute(first, "strip", pairs)
        second = lax.ppermute(second, ("track", "strip"), cross)
        base, state, alpha = call(
            functools.partial(local_kernel, cap, step_number == 0),
            [block, (3,) + block, (1, width)],
            [VMEM] * 8 + [SMEM] * 2,
            value, entry, recv, state, image, diag, lower, lower_flip, links, pos,
        )
        args = (
            base, first, second, value, recv, state, image, alpha, edge_map, coupling_flip, lower, lower_flip,
            precond_flip, maps, last_two, beyond, other, links, pos,
        )
        specs = [VMEM] * 17 + [SMEM] * 2
        if step_number < ITERS - 1:
            kernel = functools.partial(update_kernel, cap, n_track, n_strip, step_number == 0)
            image, local, begins, send = call(kernel, [block, block, chain, chunk], specs, *args)
        else:
            kernel = functools.partial(last_update_kernel, cap, n_track, n_strip)
            image, send = call(kernel, [block, (whole, 2, 128)], specs, *args)
    recv = lax.all_to_all(send, ("strip", "track"), 0, 0)
    solution, residual = call(final_kernel, [block, block], [VMEM] * 3, recv, state, image)
    return (solution[None], residual[None])


def solution(mesh):
    in_specs = (
        P("strip", "track", None),
        P("strip", "track", None, None),
        P("strip", "track", None, None),
        P("strip", "track", None, None),
        P("strip", "track", None, None),
        P("track"),
        P("strip", "track"),
    )
    out_specs = (P("strip", "track", None), P("strip", "track", None))
    return jax.shard_map(body, mesh=mesh, in_specs=in_specs, out_specs=out_specs, check_vma=False)
```

```python
import functools
import math

import jax
import jax.numpy as jnp
from jax import lax
from jax.experimental import pallas as pl
from jax.experimental.pallas import tpu as pltpu
from jax.sharding import PartitionSpec as P

ITERS = 6
CHAINS = 4
ROWS = 8
EARLY = 1
VMEM_BYTES = 16 * 1024 * 1024
PINNED = 1 << 19
NT = (((1,), (1,)), ((), ()))
NN = (((1,), (0,)), ((), ()))
VMEM = pl.BlockSpec(memory_space=pltpu.VMEM)
HBM = pl.BlockSpec(memory_space=pltpu.MemorySpace.HBM)
SMEM = pl.BlockSpec(memory_space=pltpu.SMEM)
F32 = jnp.float32


def pieces(value):
    high = value.astype(jnp.bfloat16)
    rest = value - high.astype(F32)
    middle = rest.astype(jnp.bfloat16)
    low = (rest - middle.astype(F32)).astype(jnp.bfloat16)
    return jnp.concatenate([high, middle, low], axis=0)


def split_row(row):
    return pieces(jnp.concatenate([row, row], axis=0))


def times(lhs, matrix, dims):
    out = lax.dot_general(lhs, matrix, dims, preferred_element_type=F32)
    return out[:ROWS] + out[2 * ROWS : 3 * ROWS] + out[4 * ROWS : 5 * ROWS]


def two_pieces(value):
    high = value.astype(jnp.bfloat16)
    return high, (value - high.astype(F32)).astype(jnp.bfloat16)


def times_matrix(value, matrix, dims):
    lhs = jnp.concatenate(two_pieces(value), axis=0)
    out = lax.dot_general(lhs, matrix, dims, preferred_element_type=F32)
    n = value.shape[0]
    return out[:n] + out[n:]


def product(left, right):
    high, rest = two_pieces(right)
    cross = lax.dot_general(left.astype(jnp.bfloat16), rest, NN, preferred_element_type=F32)
    return times_matrix(left, high, NN) + cross


def spread(row):
    return jnp.transpose(jnp.broadcast_to(row, (128, row.shape[1])))


def times_f32(column, matrix):
    wide = jnp.concatenate([column] * (matrix.shape[1] // 128), axis=1)
    return jnp.sum(matrix * wide, axis=0, keepdims=True)


def wide_row(ref, j):
    return jnp.broadcast_to(ref[j : j + 1, :], (ROWS, ref.shape[1]))


def is_live(pos_ref, j):
    return j < pos_ref[2]


def link(links_ref, pos_ref, j):
    joined = links_ref[0, j] if j else jnp.where(pos_ref[0] > 0, links_ref[0, 0], 0)
    return jnp.where(is_live(pos_ref, j), joined, 0).astype(F32)


def live_mask(pos_ref, shape):
    return lax.broadcasted_iota(jnp.int32, shape, 0) < pos_ref[2]


def dot_parts(residual, image):
    parts = []
    for left in (residual, image):
        partial = jnp.sum(left * image, axis=0, keepdims=True)
        parts.append(sum(partial[:, i : i + 128] for i in range(0, partial.shape[1], 128)))
    return parts


def halves(row):
    return [row[:, i : i + 128] for i in range(0, row.shape[1], 128)]


def send_ends(end, carried, first, dots, pos_ref, n_track, out_ref):
    track = pos_ref[0]
    carried = jnp.where(track % 2 == 0, carried, end)
    near = jnp.concatenate(halves(end) + dots, axis=0)
    far = jnp.concatenate(halves(carried) + dots, axis=0)
    back = jnp.concatenate(halves(first) + dots, axis=0)
    for i in range(out_ref.shape[0]):
        ahead = i % n_track - track
        out_ref[i] = jnp.where(ahead > 1, far, jnp.where(ahead == 1, near, back))


def chain_ends(state, maps_ref, last_two_ref, length):
    ends = [state[0][:1]]
    for q in range(1, CHAINS - 1):
        ends.append(state[q][:1] + times_f32(spread(ends[-1]), maps_ref[q * length + length - 1]))
    last = state[-1][:1] + times_f32(spread(state[-2][:1]), maps_ref[CHAINS * length - 1])
    ends.append(last + times_f32(spread(ends[-2]), last_two_ref[...]))
    return ends, last


def maps_kernel(
    cap, rhs_hbm, links_hbm, lower_hbm, precond_hbm, diag_hbm, coupling_hbm, pos_ref,
    maps_ref, total_ref, edge_ref, local_ref, ends_ref, begins_ref, through_ref, last_two_ref,
    lower_ref, precond_ref, diag_ref, coupling_ref,
    rhs_ref, links_ref, sems,
):
    width = lower_ref.shape[-1]
    length = cap // CHAINS
    copies = [
        pltpu.make_async_copy(rhs_hbm, rhs_ref, sems.at[0]),
        pltpu.make_async_copy(links_hbm, links_ref, sems.at[1]),
    ]

    def load(source, target, start, count):
        rows = pl.ds(start, count)
        copies.append(pltpu.make_async_copy(source.at[rows], target.at[rows], sems.at[len(copies)]))

    for begin, end in ((0, EARLY), (EARLY, length)):
        for source, target in ((lower_hbm, lower_ref), (precond_hbm, precond_ref)):
            for q in range(CHAINS):
                load(source, target, q * length + begin, end - begin)
    load(diag_hbm, diag_ref, 0, cap)
    load(coupling_hbm, coupling_ref, 0, cap)
    for copy in copies:
        copy.start()
    early = 2 + 2 * CHAINS
    for copy in copies[:early]:
        copy.wait()
    rows = lax.broadcasted_iota(jnp.int32, (width, width), 0)
    cols = lax.broadcasted_iota(jnp.int32, (width, width), 1)
    ident = jnp.where(rows == cols, 1.0, 0.0).astype(F32)
    state = [ident] * CHAINS
    local = [None] * CHAINS
    for t in range(length):
        if t == EARLY:
            for copy in copies[early:-2]:
                copy.wait()
        for q in range(CHAINS):
            j = q * length + t
            live, on = is_live(pos_ref, j), link(links_ref, pos_ref, j)
            if t == 0:
                inner = lax.dot_general(
                    ident.astype(jnp.bfloat16), lower_ref[j], NT, preferred_element_type=F32
                )
                value = lax.dot_general(
                    inner.astype(jnp.bfloat16), precond_ref[j], NT, preferred_element_type=F32
                )
            else:
                inner = times_matrix(state[q], lower_ref[j], NT)
                value = times_matrix(inner, precond_ref[j], NT)
            state[q] = jnp.where(live, -on * value, state[q])
            maps_ref[j] = state[q]
            inner = wide_row(rhs_ref, j)
            if t > 0:
                inner = inner - on * times(split_row(local[q]), lower_ref[j], NT)
            value = times(split_row(inner), precond_ref[j], NT)
            local[q] = jnp.where(live, value, local[q] if t > 0 else 0.0)
            local_ref[j : j + 1, :] = local[q][:1]
            if j == 0:
                edge_ref[...] = times_matrix(state[q], lower_ref[0], NN)
                ends_ref[1:2, :] = (on * times(split_row(local[q]), lower_ref[0], NN))[:1]
    span = 1
    while span < CHAINS:
        state = [
            state[q] if q < span else product(state[q - span], state[q])
            for q in range(CHAINS)
        ]
        if span == 1:
            last_two_ref[...] = state[-1]
        span *= 2
    for q in range(CHAINS - 1):
        through_ref[q] = state[q]
    total_ref[...] = state[-1]
    ends, _ = chain_ends(local, maps_ref, last_two_ref, length)
    ends_ref[0:1, :] = ends[-1]
    begins_ref[...] = jnp.concatenate(ends, axis=0)
    for copy in copies[-2:]:
        copy.wait()


def pair_kernel(n_track, total_ref, other_ref, ends_ref, last_two_ref, pos_ref, *refs):
    chip_ref, beyond_ref, send_ref = refs[-3:]
    first_core = pos_ref[0] % 2 == 0
    own, other = total_ref[...], other_ref[...]
    early, late = jnp.where(first_core, own, other), jnp.where(first_core, other, own)
    chip_ref[...] = product(early, late)
    dots = []
    end = ends_ref[0:1, :]
    carried = times_f32(spread(end), other_ref[...])
    send_ends(end, carried, ends_ref[1:2, :], dots, pos_ref, n_track, send_ref)
    beyond_ref[...] = product(last_two_ref[...], other_ref[...])


def chip_map(chip_refs, pos_ref, i):
    mine, paired = chip_refs[i // 2][...], chip_refs[i // 2 + len(chip_refs) // 2][...]
    return jnp.where(pos_ref[0] % 2 == i % 2, mine, paired)


def fold_kernel(cap, chips, coupling_ref, other_ref, pos_ref, *refs):
    chip_refs, (flip_ref, *out_refs) = refs[: chips - 2], refs[chips - 2 :]
    flip_kernel(cap, coupling_ref, flip_ref)
    value = None
    for i, out_ref in enumerate(out_refs):
        nearer = chip_map(chip_refs, pos_ref, i)
        if value is None:
            value = jnp.where(pos_ref[0] % 2 == 1, product(nearer, other_ref[...]), nearer)
        else:
            value = product(nearer, value)
        out_ref[...] = value


def direction_kernel(cap, n_track, folded, recv_ref, local_ref, begins_ref, maps_ref, through_ref, other_ref, coupling_ref, *refs):
    chip_refs, (pos_ref, value_ref, first_ref, second_ref, entry_ref) = refs[:-5], refs[-5:]
    track, strip = pos_ref[0], pos_ref[1]
    width = local_ref.shape[1]
    length = cap // CHAINS
    half = width // 128
    base = strip * n_track if recv_ref.shape[0] > n_track else 0
    chip = track // 2

    def chunk(index, valid):
        got = recv_ref[base + jnp.clip(index, 0, n_track - 1)]
        got = jnp.where(valid, got, 0.0)
        return jnp.concatenate([got[h : h + 1] for h in range(half)], axis=1)

    def chip_end(i):
        valid = chip - i >= 0
        return chunk(2 * (chip - i), valid) + chunk(2 * (chip - i) + 1, valid)

    furthest = n_track // 2 - 1
    if folded:
        entry = chip_end(1)
        inside = chunk(track - 1, track > 0) + times_f32(spread(entry), other_ref[...])
        entry = jnp.where(track % 2 == 1, inside, entry)
        for i in range(2, furthest + 1):
            entry = entry + times_f32(spread(chip_end(i)), chip_refs[i - 2][...])
    else:
        entry = chip_end(furthest)
        for i in range(furthest - 1, 0, -1):
            entry = chip_end(i) + times_f32(spread(entry), chip_map(chip_refs, pos_ref, i - 1))
        inside = chunk(track - 1, track > 0) + times_f32(spread(entry), other_ref[...])
        entry = jnp.where(track % 2 == 1, inside, entry)
    entry_ref[...] = entry
    columns = [spread(entry)]
    for q in range(1, CHAINS):
        begin = begins_ref[q - 1 : q, :] + times_f32(columns[0], through_ref[q - 1])
        columns.append(spread(begin))
    even = strip % 2 == 0
    for j in range(cap):
        value = local_ref[j : j + 1, :] + times_f32(columns[j // length], maps_ref[j])
        masked = jnp.where(is_live(pos_ref, j), value, 0.0)
        value_ref[j : j + 1, :] = masked
        crossed = times(split_row(jnp.broadcast_to(masked, (ROWS, width))), coupling_ref[j], NN)[:1]
        first_ref[j : j + 1, :] = jnp.where(even, masked, crossed)
        second_ref[j : j + 1, :] = jnp.where(even, crossed, masked)


def flip_kernel(cap, *refs):
    sources, targets = refs[: len(refs) // 2], refs[len(refs) // 2 :]
    for source, target in zip(sources, targets):
        for j in range(cap):
            target[j] = jnp.transpose(source[j])


def alpha_of(recv_ref):
    total = jnp.sum(recv_ref[...], axis=0)
    inner = jnp.sum(total[-2:-1], axis=1, keepdims=True)
    energy = jnp.sum(total[-1:], axis=1, keepdims=True)
    return inner / (energy + 1e-6)


def local_kernel(
    cap, first, value_ref, entry_ref, recv_ref, state_ref, image_ref, diag_ref, lower_ref,
    lower_flip_ref, links_ref, pos_ref, base_ref, next_ref, alpha_ref,
):
    width = value_ref.shape[1]
    on = [link(links_ref, pos_ref, j) for j in range(cap)]
    lowered = on[0] * times(split_row(wide_row(entry_ref, 0)), lower_flip_ref[0], NN)
    held = None
    for j in range(cap):
        lhs = split_row(wide_row(value_ref, j))
        own = times(lhs, diag_ref[j], NT) + lowered
        if j > 0:
            held = held + on[j] * times(lhs, lower_ref[j], NN)
            base_ref[j - 1 : j, :] = held[:1]
        if j < cap - 1:
            lowered = on[j + 1] * times(lhs, lower_flip_ref[j + 1], NN)
        held = own
    base_ref[cap - 1 : cap, :] = held[:1]
    if first:
        next_ref[0] = jnp.where(live_mask(pos_ref, (cap, width)), state_ref[...], 0.0)
        next_ref[1] = value_ref[...]
        next_ref[2] = jnp.zeros_like(value_ref[...])
        alpha_ref[...] = jnp.zeros((1, width), F32)
    else:
        alpha = alpha_of(recv_ref)
        next_ref[0] = state_ref[0] - alpha * image_ref[...]
        next_ref[1] = state_ref[1] - alpha * value_ref[...]
        next_ref[2] = state_ref[2] + alpha * state_ref[1]
        alpha_ref[...] = jnp.broadcast_to(alpha, (1, width))


def update_kernel(
    cap, n_track, n_strip, first, base_ref, first_ref, second_ref, value_ref, recv_ref, state_ref, image_ref, alpha_ref,
    edge_map_ref, coupling_flip_ref, lower_ref, lower_flip_ref, precond_flip_ref, maps_ref, last_two_ref, beyond_ref, other_ref, links_ref, pos_ref,
    next_ref, local_ref, begins_ref, send_ref,
):
    track, strip, count = pos_ref[0], pos_ref[1], pos_ref[2]
    width = base_ref.shape[1]
    length = cap // CHAINS
    odd = strip % 2 == 1
    one, two = first_ref[...], second_ref[...]
    below = jnp.where(strip > 0, jnp.where(odd, one, two), 0.0)
    above = jnp.where(strip < n_strip - 1, jnp.where(odd, two, one), 0.0)
    base = strip * n_track if recv_ref.shape[0] > n_track else 0
    ahead = recv_ref[base + jnp.minimum(track + 1, n_track - 1)]
    ahead = jnp.concatenate([ahead[h : h + 1] for h in range(width // 128)], axis=1)
    ahead = ahead + times_f32(spread(value_ref[pl.ds(count - 1, 1), :]), edge_map_ref[...])
    ahead = jnp.where(track < n_track - 1, ahead, 0.0)
    at_end = lax.broadcasted_iota(jnp.int32, (cap, width), 0) == count - 1
    known = base_ref[...] + above + jnp.where(at_end, ahead, 0.0)
    alpha = wide_row(alpha_ref, 0)

    def image_row(j):
        row = wide_row(known, j) + times(split_row(wide_row(below, j)), coupling_flip_ref[j], NN)
        row = jnp.where(is_live(pos_ref, j), row, 0.0)
        row = row if first else wide_row(image_ref, j) - alpha * row
        next_ref[j : j + 1, :] = row[:1]
        return row

    state = [None] * CHAINS
    rows = [image_row(q * length) for q in range(CHAINS)]
    for t in range(length):
        if local_ref is not None and t > 0:
            for q in range(CHAINS):
                j = q * length + t
                lowered = times(split_row(state[q]), lower_flip_ref[j], NN)
                rows[q] = rows[q] - link(links_ref, pos_ref, j) * lowered
        later = [image_row(q * length + t + 1) for q in range(CHAINS)] if t + 1 < length else []
        for q in range(0 if local_ref is None else CHAINS):
            j = q * length + t
            value = times(split_row(rows[q]), precond_flip_ref[j], NN)
            state[q] = jnp.where(is_live(pos_ref, j), value, state[q] if t > 0 else 0.0)
            local_ref[j : j + 1, :] = state[q][:1]
            if j == 0:
                edge = link(links_ref, pos_ref, 0) * times(split_row(state[q]), lower_ref[0], NN)
        rows = later
    dots = dot_parts(state_ref[0], next_ref[...])
    if local_ref is None:
        packed = jnp.concatenate(dots, axis=0)
        for i in range(send_ref.shape[0]):
            send_ref[i] = packed
        return
    ends, last = chain_ends(state, maps_ref, last_two_ref, length)
    begins_ref[...] = jnp.concatenate(ends, axis=0)
    carried = times_f32(spread(last), other_ref[...]) + times_f32(spread(ends[-3]), beyond_ref[...])
    send_ends(ends[-1], carried, edge[:1], dots, pos_ref, n_track, send_ref)


def last_update_kernel(cap, n_track, n_strip, *refs):
    update_kernel(cap, n_track, n_strip, False, *refs[:-1], None, None, refs[-1])


def final_kernel(recv_ref, state_ref, image_ref, solution_ref, residual_ref):
    alpha = alpha_of(recv_ref)
    solution_ref[...] = state_ref[2] + alpha * state_ref[1]
    residual_ref[...] = state_ref[0] - alpha * image_ref[...]


def call(kernel, outs, specs, *args, scratch=(), vmem=VMEM_BYTES):
    outs = [out if len(out) == 2 and isinstance(out[0], tuple) else (out, F32) for out in outs]
    args = [
        pltpu.with_memory_space_constraint(arg, spec.memory_space) if arg.size >= PINNED or spec is HBM else arg
        for arg, spec in zip(args, specs)
    ]
    return pl.pallas_call(
        kernel,
        out_shape=[
            pltpu.VMEM(shape, dtype) if math.prod(shape) >= PINNED else jax.ShapeDtypeStruct(shape, dtype)
            for shape, dtype in outs
        ],
        in_specs=specs,
        out_specs=[VMEM] * len(outs),
        scratch_shapes=scratch,
        compiler_params=pltpu.CompilerParams(vmem_limit_bytes=vmem),
    )(*args)


def body(rhs, principal_tiles, lower_blocks, coupling_blocks, precond_blocks, seg_blocks, links):
    cap, width = rhs.shape[1:]
    n_track, n_strip = lax.axis_size("track"), lax.axis_size("strip")
    track, strip = lax.axis_index("track"), lax.axis_index("strip")
    pos = jnp.stack([track, strip, seg_blocks[0]]).astype(jnp.int32)
    rhs = rhs[0]
    whole = n_track * n_strip
    chips = n_track // 2
    block = (cap, width)
    square = (width, width)
    stack = (cap, width, width)
    chunk = (whole, width // 128 + 2, 128)
    chain = (CHAINS, width)
    swap = [(i, i ^ 1) for i in range(n_track)]

    def flip(*stacks):
        kernel = functools.partial(flip_kernel, cap)
        return call(kernel, [(stack, jnp.bfloat16)] * len(stacks), [VMEM] * len(stacks), *stacks)

    maps, total, edge_map, local, ends, begins, through, last_two, lower, precond, diag, coupling = call(
        functools.partial(maps_kernel, cap),
        [stack, square, square, block, (2, width), chain, (CHAINS - 1,) + square, square] + [(stack, jnp.bfloat16)] * 4,
        [HBM] * 6 + [SMEM],
        rhs, links, lower_blocks[0], precond_blocks[0], principal_tiles[0], coupling_blocks[0], pos,
        scratch=[
            pltpu.VMEM(block, F32), pltpu.SMEM(links.shape, jnp.int32),
            pltpu.SemaphoreType.DMA((4 * CHAINS + 4,)),
        ],
    )
    other = lax.ppermute(total, "track", swap)
    lower_flip, precond_flip = flip(lower, precond)
    chip, beyond, send = call(
        functools.partial(pair_kernel, n_track),
        [square, square, (n_track, width // 128, 128)],
        [VMEM] * 4 + [SMEM] + [VMEM] * 6,
        total, other, ends, last_two, pos, maps, lower, lower_flip, precond_flip, diag, coupling,
    )
    nearer = []
    for k in range(1, chips - 1, 2):
        shifted = swap[:2]
        for i in range(2, n_track):
            shifted = shifted + [(i, 2 + (i - 2 + 2 * (k + i % 2)) % (n_track - 2))]
        nearer.append(lax.ppermute(chip, "track", shifted))

    state = image = rhs
    pairs = [(i, i ^ 1) for i in range(n_strip) if i ^ 1 < n_strip]
    cross = []
    for d in range(n_track):
        for i in range(n_strip):
            partner = i + 1 if i % 2 else i - 1
            if 0 <= partner < n_strip:
                cross.append((d * n_strip + i, d * n_strip + partner))
            else:
                cross.append((d * n_strip + i, (d ^ 1) * n_strip + i))
    for step_number in range(ITERS):
        recv = lax.all_to_all(send, ("strip", "track") if step_number else "track", 0, 0)
        if step_number == 0:
            recv, edge_map, coupling, *nearer = lax.optimization_barrier((recv, edge_map, coupling, *nearer))
            edge_map = lax.ppermute(edge_map, "track", [((i + 1) % n_track, i) for i in range(n_track)])
            nearer += [lax.ppermute(part, "track", swap) for part in nearer]
        value, first, second, entry = call(
            functools.partial(direction_kernel, cap, n_track, step_number > 0),
            [block, block, block, (1, width)],
            [VMEM] * (7 + len(nearer)) + [SMEM],
            recv, local, begins, maps, through, other, coupling, *nearer, pos,
        )
        if step_number == 0:
            coupling_flip, *nearer = call(
                functools.partial(fold_kernel, cap, chips),
                [(stack, jnp.bfloat16)] + [square] * (chips - 2),
                [VMEM] * 2 + [SMEM] + [VMEM] * len(nearer),
                coupling, other, pos, *nearer,
            )
        first = lax.ppermute(first, "strip", pairs)
        second = lax.ppermute(second, ("track", "strip"), cross)
        base, state, alpha = call(
            functools.partial(local_kernel, cap, step_number == 0),
            [block, (3,) + block, (1, width)],
            [VMEM] * 8 + [SMEM] * 2,
            value, entry, recv, state, image, diag, lower, lower_flip, links, pos,
        )
        args = (
            base, first, second, value, recv, state, image, alpha, edge_map, coupling_flip, lower, lower_flip,
            precond_flip, maps, last_two, beyond, other, links, pos,
        )
        specs = [VMEM] * 17 + [SMEM] * 2
        if step_number < ITERS - 1:
            kernel = functools.partial(update_kernel, cap, n_track, n_strip, step_number == 0)
            image, local, begins, send = call(kernel, [block, block, chain, chunk], specs, *args)
        else:
            kernel = functools.partial(last_update_kernel, cap, n_track, n_strip)
            image, send = call(kernel, [block, (whole, 2, 128)], specs, *args)
    recv = lax.all_to_all(send, ("strip", "track"), 0, 0)
    solution, residual = call(final_kernel, [block, block], [VMEM] * 3, recv, state, image)
    return (solution[None], residual[None])


def solution(mesh):
    in_specs = (
        P("strip", "track", None),
        P("strip", "track", None, None),
        P("strip", "track", None, None),
        P("strip", "track", None, None),
        P("strip", "track", None, None),
        P("track"),
        P("strip", "track"),
    )
    out_specs = (P("strip", "track", None), P("strip", "track", None))
    return jax.shard_map(body, mesh=mesh, in_specs=in_specs, out_specs=out_specs, check_vma=False)
```
